32 devices in a mesh: dp: 4 (over x, core), row: 4 (over z), col: 2 (over y).
Axes of the slice: x: 2, y: 2, z: 4, core: 2. Of those that a mesh axis runs over, the one named last changes fastest.
Arguments:
- hidden_in: bfloat16 [8192, 1024], P(('dp', 'col'), 'row'), may hold values from -6 to 6
- norm1_gain: float32 [1024], P('row'), may hold values from 0.25 to 1.75
- query_weight: bfloat16 [1024, 1024], P('row', 'col'), may hold values from -0.75 to 0.75
- key_weight: bfloat16 [1024, 512], P('row', 'col'), may hold values from -0.75 to 0.75
- value_weight: bfloat16 [1024, 512], P('row', 'col'), may hold values from -0.1875 to 0.1875
- output_weight: bfloat16 [1024, 1024], P('col', 'row'), may hold values from -0.375 to 0.375
- norm2_gain: float32 [1024], P('row'), may hold values from 0.25 to 1.75
- router_weight: bfloat16 [1024, 32], P('row'), may hold values from -0.09375 to 0.09375
- gate_weight: bfloat16 [32, 1024, 512], P(None, 'row', 'col'), may hold values from -0.1875 to 0.1875
- up_weight: bfloat16 [32, 1024, 512], P(None, 'row', 'col'), may hold values from -0.1875 to 0.1875
- down_weight: bfloat16 [32, 512, 1024], P(None, 'col', 'row'), may hold values from -1 to 1
- segment_ids: int32 [16, 512], P('dp'), may hold values from 0 to 3, never falling along the last dimension, each value on 1 to 256 neighbouring positions
- expert_ids: int32 [8192, 8], P('dp'), may hold values from 0 to 31, all different within a row; in each aligned block of 2048 rows (0 to 2047, 2048 to 4095, ...) at most 640 rows name the same one
- grad_out: bfloat16 [8192, 1024], P(('dp', 'col'), 'row'), may hold values from -6 to 6
Outputs:
- mixed_out: bfloat16 [8192, 1024], P(('dp', 'col'), 'row')
- grad_in: float32 [8192, 1024], P(('dp', 'col'), 'row')
- grad_norm1: float32 [1024], P('row')
- grad_query: float32 [1024, 1024], P('row', 'col')
- grad_key: float32 [1024, 512], P('row', 'col')
- grad_value: float32 [1024, 512], P('row', 'col')
- grad_output: float32 [1024, 1024], P('col', 'row')
- grad_norm2: float32 [1024], P('row')
- grad_router: float32 [1024, 32], P('row')
- grad_gate: float32 [32, 1024, 512], P('dp', 'row', 'col')
- grad_up: float32 [32, 1024, 512], P('dp', 'row', 'col')
- grad_down: float32 [32, 512, 1024], P('dp', 'col', 'row')
The draws below stay inside these ranges and needn't reach their ends.
Inputs may be any that keep to these rules, and one draw needn't show every extreme that they name: `segment_ids`: segment numbers never fall along a sequence; each document has at most 256 tokens. `expert_ids`: each row names 8 different experts; among the 2048 rows of one index of dp no expert is named more than 640 times, a bound that some block reaches.
All inputs are finite; a program needn't handle non-finite values.
Results may differ from the reference program's by a relative error of at most 0.02.
Values may be sent and summed in bfloat16 or wider, within the bound.
No kernel may reach another device: no remote copies, remote signals or barrier semaphores. Data moves between devices by JAX's collectives and lax.ppermute only.
A program may use at most 256 MiB of HBM per device.

```python
import math
import jax
import jax.numpy as jnp
import numpy as np
from jax import lax

D = 1024
HEADS = 16
KV_HEADS = 8
HEAD_DIM = 64
EXPERTS = 32
TOP_K = 8
EXPERT_HIDDEN = 512
SEQ_LEN = 512
GROUP = 2048
TOKENS = 8192
SEQS = 16
CAP = 640


def block_levels(rng, extent, shards, least, largest):
    level, own = 1.0, jax.random.fold_in(rng, 6)
    for dim, parts in shards:
        draws = jnp.exp(jax.random.uniform(jax.random.fold_in(own, dim), (parts,), jnp.float32, least / len(shards), largest / len(shards)))
        level = level * jnp.repeat(draws, extent[dim] // parts).reshape([-1 if axis == dim else 1 for axis in range(len(extent))])
    return level


def split_up(number_of, total, most, lean):
    loads = [(1 << 20) // math.isqrt(rank ** lean) + 1 for rank in range(2, number_of + 1)]
    rest, given = total - most - (number_of - 1), [1] * (number_of - 1)
    while rest > 0:
        candidates = [i for i in range(number_of - 1) if given[i] < most]
        mass, budget = sum([loads[i] for i in candidates]), rest
        for i in candidates:
            addition = min(most - given[i], max(1, budget * loads[i] // mass), rest)
            given[i] = given[i] + addition
            rest = rest - addition
    return np.array([most] + given)


def ragged(rng, count, total, reach, lean):
    if count == 2:
        one = jax.random.randint(rng, (), max(1, total - reach), min(reach, total - 1) + 1)
        return jnp.stack([one, total - one])
    lengths = jnp.asarray(split_up(count, total, reach, lean), jnp.int32)
    couples = (count - 1) // 2
    source_of, sink = lengths[1:1 + 2 * couples:2], lengths[2:2 + 2 * couples:2]
    slack = jnp.minimum(source_of - 1, reach - sink)
    shifted = jax.random.randint(jax.random.fold_in(rng, 1), (couples,), 0, 1 << 20) % (slack + 1)
    lengths = lengths.at[1:1 + 2 * couples:2].set(source_of - shifted).at[2:2 + 2 * couples:2].set(sink + shifted)
    return lengths[jax.random.permutation(jax.random.fold_in(rng, 2), count)]


def deal_out(own_key, own, number, rows, amount, top, reach, slope):
    order = jax.random.permutation(own_key, amount)
    heavy_load, common = portions_of(amount, rows * top, reach, slope, True), portions_of(amount, rows * top, reach, slope, False)
    places = jnp.arange(amount)

    def named(tallies, rotation):
        used = int((tallies > 0).sum())
        fixed = max(1, used // 4)
        shifted = fixed + (places - fixed + rotation * (used - fixed)) % max(1, amount - fixed)
        return jnp.zeros((amount,), jnp.int32).at[order[jnp.where(places < fixed, places, shifted)]].set(jnp.asarray(tallies, jnp.int32))

    tallies = jnp.where(number % 4 == 0, named(heavy_load, number // 4), named(common, number - number // 4 - 1))
    mixed = jax.random.permutation(jax.random.fold_in(own, 3), amount)
    giver, sink = mixed[0:amount // 2 * 2:2], mixed[1:amount // 2 * 2:2]
    slack = jnp.minimum(tallies[giver] - 1, reach - tallies[sink]) // 2
    slack = jnp.where((giver == order[0]) | (sink == order[0]) | (tallies[sink] == 0), 0, jnp.maximum(slack, 0))
    shifted = jax.random.randint(jax.random.fold_in(own, 4), (amount // 2,), 0, 1 << 20) % (slack + 1)
    tallies = tallies.at[giver].add(-shifted).at[sink].add(shifted)
    members = jnp.searchsorted(jnp.cumsum(tallies), jnp.arange(rows * top), side="right").astype(jnp.int32)
    table = members.reshape(top, rows).T
    table = table[jax.random.permutation(jax.random.fold_in(own, 1), rows)]
    rotation = jax.random.randint(jax.random.fold_in(own, 2), (rows, 1), 0, top)
    return jnp.take_along_axis(table, (jnp.arange(top)[None, :] + rotation) % top, axis=1)


def portions_of(number_of, total, reach, skew, full):
    portions = [(1 << 20) // math.isqrt(grade ** skew) + 1 for grade in range(1, number_of + 1)]
    largest = reach if full else min(reach, max(-(-total // number_of), total * portions[0] // sum(portions)))
    least = 1 if total - largest >= number_of - 1 else 0
    holding, rest = [largest] + [least] * (number_of - 1), total - largest - least * (number_of - 1)
    while rest > 0:
        free = [i for i in range(1, number_of) if holding[i] < largest] or [i for i in range(1, number_of) if holding[i] < reach]
        whole, remaining = sum([portions[i] for i in free]), rest
        for i in free:
            more = min(reach - holding[i], max(1, remaining * portions[i] // whole), rest)
            holding[i] = holding[i] + more
            rest = rest - more
    return np.array(holding)


def scatter_about(key, shape, spread, most, pieces=(), kind=jnp.bfloat16):
    entries = spread * jax.random.normal(key, shape, jnp.float32)
    if pieces:
        entries = entries * block_levels(key, shape, pieces, -0.22, 0.18)
    return jnp.clip(entries, -most, most).astype(kind)


def setup_inputs(seed: int = 0) -> dict:
    splits = jax.random.split(jax.random.key(seed), 15)
    hidden_in = scatter_about(splits[0], (TOKENS, D), 1.0, 6.0, ((0, 8), (1, 4)))
    norm1_gain = jnp.clip(1.0 + 0.15 * jax.random.normal(splits[1], (D,), jnp.float32), 0.25, 1.75)
    query_weight = scatter_about(splits[2], (D, HEADS * HEAD_DIM), (D // 16) ** -0.5, 0.75, ((0, 4), (1, 2)))
    key_weight = scatter_about(splits[3], (D, KV_HEADS * HEAD_DIM), (D // 16) ** -0.5, 0.75, ((0, 4), (1, 2)))
    value_weight = scatter_about(splits[4], (D, KV_HEADS * HEAD_DIM), D ** -0.5, 0.1875, ((0, 4), (1, 2)))
    output_weight = scatter_about(splits[5], (HEADS * HEAD_DIM, D), (HEADS * HEAD_DIM // 4) ** -0.5, 0.375, ((0, 2), (1, 4)))
    norm2_gain = jnp.clip(1.0 + 0.15 * jax.random.normal(splits[6], (D,), jnp.float32), 0.25, 1.75)
    router_weight = scatter_about(splits[7], (D, EXPERTS), (4 * D) ** -0.5, 0.09375, ((0, 4),))
    gate_weight = scatter_about(splits[8], (EXPERTS, D, EXPERT_HIDDEN), D ** -0.5, 0.1875, ((1, 4), (2, 2)))
    up_weight = scatter_about(splits[9], (EXPERTS, D, EXPERT_HIDDEN), D ** -0.5, 0.1875, ((1, 4), (2, 2)))
    down_weight = scatter_about(splits[10], (EXPERTS, EXPERT_HIDDEN, D), (EXPERT_HIDDEN // 16) ** -0.5, 1.0, ((1, 2), (2, 4)))
    segment_ids = jax.vmap(lambda own: jnp.searchsorted(jnp.cumsum(ragged(own, 4, SEQ_LEN, SEQ_LEN // 2, 2)), jnp.arange(SEQ_LEN), side="right"))(jax.random.split(splits[11], SEQS)).reshape((SEQS, SEQ_LEN)).astype(jnp.int32)
    expert_ids_keys = jax.random.split(jax.random.fold_in(splits[12], 1), TOKENS // GROUP)
    expert_ids_turns = jax.random.permutation(jax.random.fold_in(splits[12], 3), TOKENS // GROUP)
    expert_ids = jax.vmap(lambda own, number: deal_out(jax.random.fold_in(splits[12], 2), own, number, GROUP, EXPERTS, TOP_K, CAP, 1))(expert_ids_keys, expert_ids_turns).reshape((TOKENS, TOP_K))
    grad_out = scatter_about(splits[13], (TOKENS, D), 1.0, 6.0, ((0, 8), (1, 4)))
    return dict(hidden_in=hidden_in, norm1_gain=norm1_gain, query_weight=query_weight, key_weight=key_weight, value_weight=value_weight, output_weight=output_weight, norm2_gain=norm2_gain, router_weight=router_weight, gate_weight=gate_weight, up_weight=up_weight, down_weight=down_weight, segment_ids=segment_ids, expert_ids=expert_ids, grad_out=grad_out)


epsilon = 1e-06
rope_base = 10000.0
masked_score = -1e+30

@jax.custom_vjp
def low(v):
    return lax.optimization_barrier(v.astype(jnp.bfloat16)).astype(jnp.float32)

@jax.custom_vjp
def low_back(v):
    return v

def low_keep(v):
    return (low(v), None)

def low_pass(kept, grad):
    return (grad,)

def back_keep(v):
    return (v, None)

def back_low(kept, grad):
    return (low(grad),)
low.defvjp(low_keep, low_pass)
low_back.defvjp(back_keep, back_low)

def rope_tables(seq_len, head_dim):
    midpoint = head_dim // 2
    frequency = rope_base ** (-2.0 * jnp.arange(midpoint, dtype=jnp.float32) / head_dim)
    angles = jnp.arange(seq_len, dtype=jnp.float32)[:, None] * frequency[None, :]
    return (jnp.cos(angles), jnp.sin(angles))

def rotate(values, cosines, sines):
    midpoint = values.shape[-1] // 2
    first = values[..., :midpoint]
    second = values[..., midpoint:]
    return jnp.concatenate([first * cosines - second * sines, second * cosines + first * sines], -1)

def block_mask(segments):
    positions = jnp.arange(segments.shape[0], dtype=jnp.int32)
    return (positions[None, :] <= positions[:, None]) & (segments[None, :] == segments[:, None])

def slot_tables(expert_ids, capacity, experts):
    count_rows, chosen = expert_ids.shape
    assigned = count_rows * chosen
    flat_ids = expert_ids.reshape(-1)
    member = (flat_ids[:, None] == jnp.arange(experts, dtype=jnp.int32)[None, :]).astype(jnp.int32)
    earlier = jnp.cumsum(member, 0) - member
    place = lax.optimization_barrier(jnp.sum(earlier * member, 1))
    slot_of = flat_ids * capacity + place
    owner = jnp.full((experts * capacity,), assigned, jnp.int32).at[slot_of].set(jnp.arange(assigned, dtype=jnp.int32))
    filled = owner < assigned
    token_of = jnp.where(filled, owner // chosen, 0)
    return (slot_of.reshape(count_rows, chosen), owner, filled, token_of)

def rms_norm(values, gain):
    inv_rms = lax.rsqrt(lax.optimization_barrier(jnp.mean(values * values, -1, keepdims=True)) + epsilon)
    return values * inv_rms * gain

def attend(block):
    query, key, value, segments = block
    products = low_back(jnp.einsum('qgjd,kgd->gjqk', query, key, precision=lax.Precision.HIGHEST))
    scores = jnp.where(block_mask(segments), products * (1.0 / HEAD_DIM), masked_score)
    row_max = lax.optimization_barrier(jnp.max(scores, -1, keepdims=True))
    powers = jnp.exp(scores - row_max)
    attention = low(powers / lax.optimization_barrier(jnp.sum(powers, -1, keepdims=True)))
    return jnp.einsum('gjqk,kgd->qgjd', attention, value, precision=lax.Precision.HIGHEST)

def group_forward(params, residual, segments, expert_ids):
    norm1_gain, query_weight, key_weight, value_weight, output_weight, norm2_gain, router_weight, gate_weight, up_weight, down_weight = params
    highest = lax.Precision.HIGHEST
    sequences = GROUP // SEQ_LEN
    ratio = HEADS // KV_HEADS
    cosines, sines = rope_tables(SEQ_LEN, HEAD_DIM)
    normed_one = low(rms_norm(residual, norm1_gain))
    query_raw = low_back(jnp.dot(normed_one, query_weight, precision=highest))
    key_raw = low_back(jnp.dot(normed_one, key_weight, precision=highest))
    value_low = low(low_back(jnp.dot(normed_one, value_weight, precision=highest)))
    query_low = low(rotate(query_raw.reshape(sequences, SEQ_LEN, KV_HEADS, ratio, HEAD_DIM), cosines[:, None, None, :], sines[:, None, None, :]))
    key_low = low(rotate(key_raw.reshape(sequences, SEQ_LEN, KV_HEADS, HEAD_DIM), cosines[:, None, :], sines[:, None, :]))
    value_low = value_low.reshape(sequences, SEQ_LEN, KV_HEADS, HEAD_DIM)
    attended = lax.map(jax.checkpoint(attend), (query_low, key_low, value_low, segments))
    heads_out = low(low_back(attended.reshape(GROUP, HEADS * HEAD_DIM)))
    middle = residual + low_back(jnp.dot(heads_out, output_weight, precision=highest))
    normed_two = low(rms_norm(middle, norm2_gain))
    logits = low_back(jnp.dot(normed_two, router_weight, precision=highest))
    member = (expert_ids[:, :, None] == jnp.arange(EXPERTS, dtype=jnp.int32)[None, None, :]).astype(jnp.float32)
    gates = jax.nn.softmax(lax.optimization_barrier(jnp.sum(member * logits[:, None, :], -1)), -1)
    slot_of, owner, filled, token_of = slot_tables(expert_ids, CAP, EXPERTS)
    slot_in = jnp.where(filled[:, None], normed_two[token_of], 0.0).reshape(EXPERTS, CAP, D)
    paired = jnp.concatenate([gate_weight, up_weight], 2)
    gate_up = low_back(jnp.einsum('ecd,edh->ech', slot_in, paired, precision=highest))
    hidden = low(jax.nn.silu(gate_up[..., :EXPERT_HIDDEN]) * gate_up[..., EXPERT_HIDDEN:])
    expert_out = low_back(jnp.einsum('ech,ehd->ecd', hidden, down_weight, precision=highest)).reshape(EXPERTS * CAP, D)
    routed = jnp.einsum('tk,tkd->td', gates, expert_out[slot_of], precision=highest)
    return middle + routed

def reference(hidden_in, norm1_gain, query_weight, key_weight, value_weight, output_weight, norm2_gain, router_weight, gate_weight, up_weight, down_weight, segment_ids, expert_ids, grad_out):
    params = tuple((item.astype(jnp.float32) for item in (norm1_gain, query_weight, key_weight, value_weight, output_weight, norm2_gain, router_weight, gate_weight, up_weight, down_weight)))
    groups = TOKENS // GROUP
    residual = hidden_in.astype(jnp.float32).reshape(groups, GROUP, D)
    segments = segment_ids.reshape(groups, GROUP // SEQ_LEN, SEQ_LEN)
    chosen_ids = expert_ids.reshape(groups, GROUP, TOP_K)

    def forward(weights, inputs):

        def one_group(block):
            return group_forward(weights, block[0], block[1], block[2])
        return lax.map(jax.checkpoint(one_group), (inputs, segments, chosen_ids))
    outputs, pullback = jax.vjp(forward, params, residual)
    grad_params, grad_residual = pullback(grad_out.astype(jnp.float32).reshape(groups, GROUP, D))
    return (outputs.reshape(TOKENS, D).astype(jnp.bfloat16), grad_residual.reshape(TOKENS, D), grad_params[0], grad_params[1], grad_params[2], grad_params[3], grad_params[4], grad_params[5], grad_params[6], grad_params[7], grad_params[8], grad_params[9])
```

```python
import functools

import jax
import jax.numpy as jnp
from jax import lax
from jax.experimental import pallas as pl
from jax.experimental.pallas import tpu as pltpu
from jax.sharding import PartitionSpec as P

HEAD_DIM = 64
LANES = 128

epsilon = 1e-06
rope_base = 10000.0
masked_score = -1e30

f32 = jnp.float32
bf16 = jnp.bfloat16

BIG = pltpu.CompilerParams(vmem_limit_bytes=56 * 1024 * 1024)


def dot(left, right):
    return lax.dot_general(left, right, (((1,), (0,)), ((), ())), preferred_element_type=f32)


def dot_nt(left, right):
    return lax.dot_general(left, right, (((1,), (1,)), ((), ())), preferred_element_type=f32)


def dot_tn(left, right):
    return lax.dot_general(left, right, (((0,), (0,)), ((), ())), preferred_element_type=f32)


def rope_tables(seq_len):
    midpoint = HEAD_DIM // 2
    frequency = rope_base ** (-2.0 * jnp.arange(midpoint, dtype=f32) / HEAD_DIM)
    angles = jnp.arange(seq_len, dtype=f32)[:, None] * frequency[None, :]
    cosines, sines = jnp.cos(angles), jnp.sin(angles)
    return (
        jnp.tile(cosines, (1, LANES // midpoint)),
        jnp.tile(jnp.concatenate([-sines, sines], 1), (1, LANES // HEAD_DIM)),
    )


def partner(tile):
    lane = lax.broadcasted_iota(jnp.int32, tile.shape, 1)
    half = HEAD_DIM // 2
    return jnp.where(
        (lane % HEAD_DIM) < half,
        pltpu.roll(tile, LANES - half, 1),
        pltpu.roll(tile, half, 1),
    )


def spread_pair(tile):
    tile = tile.astype(f32)
    lane = lax.broadcasted_iota(jnp.int32, tile.shape, 1)
    swapped = pltpu.roll(tile, HEAD_DIM, 1)
    low = lane < HEAD_DIM
    return (
        jnp.where(low, tile, swapped).astype(bf16),
        jnp.where(low, swapped, tile).astype(bf16),
    )


def split_heads(tile):
    lane = lax.broadcasted_iota(jnp.int32, tile.shape, 1)
    low = lane < HEAD_DIM
    zero = jnp.zeros_like(tile)
    return jnp.where(low, tile, zero), jnp.where(low, zero, tile)


def block_mask(seg_col, seg_row, start, rows, keys):
    row = lax.broadcasted_iota(jnp.int32, (rows, keys), 0) + start
    key = lax.broadcasted_iota(jnp.int32, (rows, keys), 1)
    return (key <= row) & (seg_col[start : start + rows, :] == seg_row[:, :keys])


def attend_kernel(
    query_in, key_in, value_in, cos_ref, sin_ref, col_ref, row_ref,
    query_out, key_out, value_out, heads_out, sums_out, *, block
):
    seq_len = query_in.shape[0]
    cosines, sines = cos_ref[...], sin_ref[...]
    key = key_in[...]
    key_low = (key * cosines + partner(key) * sines).astype(bf16)
    key_out[...] = key_low
    value_low = value_in[...].astype(bf16)
    value_out[...] = value_low
    keys, values = spread_pair(key_low), spread_pair(value_low)
    lane = lax.broadcasted_iota(jnp.int32, (block, LANES), 1)
    scale = 1.0 / HEAD_DIM
    for group in range(2):
        cols = slice(group * LANES, (group + 1) * LANES)
        query = query_in[:, cols]
        query_low = (query * cosines + partner(query) * sines).astype(bf16)
        query_out[:, cols] = query_low
        parts = split_heads(query_low)
        value_parts = split_heads(values[group])
        for start in range(0, seq_len, block):
            reach = start + block
            mask = block_mask(col_ref[...], row_ref[...], start, block, reach)
            total = jnp.zeros((block, LANES), f32)
            for head in range(2):
                scores = dot_nt(parts[head][start:reach], keys[group][:reach]) * scale
                scores = jnp.where(mask, scores, masked_score)
                top = jnp.max(scores, -1, keepdims=True)
                powers = jnp.exp(scores - top)
                mass = jnp.sum(powers, -1, keepdims=True)
                attention = (powers / mass).astype(bf16)
                total += dot(attention, value_parts[head][:reach])
                place = group * 2 + head
                sums = jnp.broadcast_to(top + jnp.log(mass), (block, LANES))
                if place == 0:
                    sums_out[start:reach, :] = sums
                else:
                    sums_out[start:reach, :] = jnp.where(
                        lane == place, sums, sums_out[start:reach, :]
                    )
            heads_out[start:reach, cols] = total.astype(bf16)


def attend_forward(raw, tables, seg_col, seg_row, kv_heads, block):
    seq_len = raw.shape[0]
    pairs = kv_heads // 2
    width = pairs * LANES
    spec = lambda cols, at: pl.BlockSpec((seq_len, cols), at)
    return pl.pallas_call(
        functools.partial(attend_kernel, block=block),
        grid=(pairs,),
        in_specs=[
            spec(2 * LANES, lambda i: (0, i)),
            spec(LANES, lambda i: (0, 2 * pairs + i)),
            spec(LANES, lambda i: (0, 3 * pairs + i)),
            spec(LANES, lambda i: (0, 0)),
            spec(LANES, lambda i: (0, 0)),
            pl.BlockSpec((seq_len, 1), lambda i: (0, 0)),
            pl.BlockSpec((1, seq_len), lambda i: (0, 0)),
        ],
        out_specs=[
            spec(2 * LANES, lambda i: (0, i)),
            spec(LANES, lambda i: (0, i)),
            spec(LANES, lambda i: (0, i)),
            spec(2 * LANES, lambda i: (0, i)),
            spec(LANES, lambda i: (0, i)),
        ],
        out_shape=[
            jax.ShapeDtypeStruct((seq_len, 2 * width), bf16),
            jax.ShapeDtypeStruct((seq_len, width), bf16),
            jax.ShapeDtypeStruct((seq_len, width), bf16),
            jax.ShapeDtypeStruct((seq_len, 2 * width), bf16),
            jax.ShapeDtypeStruct((seq_len, width), f32),
        ],
        compiler_params=BIG,
        name="attend_forward",
    )(raw, raw, raw, *tables, seg_col, seg_row)


def attend_back_kernel(
    query_in, key_in, value_in, sums_in, grad_in, cos_ref, sin_ref, col_ref, row_ref,
    query_out, key_out, value_out, key_sum, value_sum, *, block
):
    seq_len = query_in.shape[0]
    keys, values = spread_pair(key_in[...]), spread_pair(value_in[...])
    lane = lax.broadcasted_iota(jnp.int32, (seq_len, LANES), 1)
    low = lane < HEAD_DIM
    scale = 1.0 / HEAD_DIM
    folded = []
    for group in range(2):
        cols = slice(group * LANES, (group + 1) * LANES)
        query_parts = split_heads(query_in[:, cols])
        grad_parts = split_heads(grad_in[:, cols])
        key_parts = split_heads(keys[group])
        key_sum[...] = jnp.zeros_like(key_sum)
        value_sum[...] = jnp.zeros_like(value_sum)
        for start in range(0, seq_len, block):
            reach = start + block
            rows = slice(start, reach)
            mask = block_mask(col_ref[...], row_ref[...], start, block, reach)
            total = jnp.zeros((block, LANES), f32)
            for head in range(2):
                place = group * 2 + head
                query, grad = query_parts[head][rows], grad_parts[head][rows]
                scores = dot_nt(query, keys[group][:reach]) * scale
                powers = jnp.exp(scores - sums_in[rows, place : place + 1])
                attention = jnp.where(mask, powers, 0.0)
                value_sum[:reach, :] += dot_tn(attention.astype(bf16), grad)
                grad_probs = dot_nt(grad, values[group][:reach])
                inner = jnp.sum(grad_probs * attention, -1, keepdims=True)
                grad_scores = (attention * (grad_probs - inner) * scale).astype(bf16)
                key_sum[:reach, :] += dot_tn(grad_scores, query)
                total += dot(grad_scores, key_parts[head][:reach])
            cosines, sines = cos_ref[rows, :], sin_ref[rows, :]
            query_out[rows, cols] = (total * cosines - partner(total) * sines).astype(bf16)
        grad_key, grad_value = key_sum[...], value_sum[...]
        folded.append(
            (
                grad_key + pltpu.roll(grad_key, HEAD_DIM, 1),
                grad_value + pltpu.roll(grad_value, HEAD_DIM, 1),
            )
        )
    grad_key = jnp.where(low, folded[0][0], folded[1][0])
    grad_value = jnp.where(low, folded[0][1], folded[1][1])
    key_out[...] = (grad_key * cos_ref[...] - partner(grad_key) * sin_ref[...]).astype(bf16)
    value_out[...] = grad_value.astype(bf16)


def attend_backward(query, key, value, sums, grad, tables, seg_col, seg_row, block):
    seq_len = query.shape[0]
    width = key.shape[1]
    pairs = width // LANES
    spec = lambda cols, at: pl.BlockSpec((seq_len, cols), at)
    here = lambda i: (0, i)
    first = lambda i: (0, 0)
    return pl.pallas_call(
        functools.partial(attend_back_kernel, block=block),
        grid=(pairs,),
        in_specs=[
            spec(2 * LANES, here),
            spec(LANES, here),
            spec(LANES, here),
            spec(LANES, here),
            spec(2 * LANES, here),
            spec(LANES, first),
            spec(LANES, first),
            pl.BlockSpec((seq_len, 1), first),
            pl.BlockSpec((1, seq_len), first),
        ],
        out_specs=[spec(2 * LANES, here), spec(LANES, here), spec(LANES, here)],
        out_shape=[
            jax.ShapeDtypeStruct((seq_len, 2 * width), bf16),
            jax.ShapeDtypeStruct((seq_len, width), bf16),
            jax.ShapeDtypeStruct((seq_len, width), bf16),
        ],
        scratch_shapes=[pltpu.VMEM((seq_len, LANES), f32), pltpu.VMEM((seq_len, LANES), f32)],
        compiler_params=BIG,
        name="attend_backward",
    )(query, key, value, sums, grad, *tables, seg_col, seg_row)


def dispatch_kernel(place_ref, *refs, capacity):
    out_ref = refs[-1]
    place = place_ref[0]
    slots = lax.broadcasted_iota(jnp.int32, (capacity, place.shape[1]), 0)
    chosen = jnp.where(slots == place, 1.0, 0.0).astype(bf16)
    start = 0
    for ref in refs[:-1]:
        for part in range(ref.shape[0]):
            width = ref.shape[2]
            out_ref[0, :, start : start + width] = dot(chosen, ref[part]).astype(bf16)
            start += width


def dispatch(places, pieces, capacity):
    count, _, tokens = places.shape
    width = sum(piece.shape[0] * piece.shape[2] for piece in pieces)
    return pl.pallas_call(
        functools.partial(dispatch_kernel, capacity=capacity),
        grid=(count,),
        in_specs=[pl.BlockSpec((1, 1, tokens), lambda i: (i, 0, 0))]
        + [pl.BlockSpec(piece.shape, lambda i: (0, 0, 0)) for piece in pieces],
        out_specs=pl.BlockSpec((1, capacity, width), lambda i: (i, 0, 0)),
        out_shape=jax.ShapeDtypeStruct((count, capacity, width), bf16),
        compiler_params=BIG,
        name="dispatch_rows",
    )(places, *pieces)


def picks(place_ref, count, capacity):
    rows = place_ref.shape[0]
    slots = lax.broadcasted_iota(jnp.int32, (rows, capacity), 1)
    return jnp.concatenate(
        [
            jnp.where(slots == place_ref[:, part : part + 1], 1.0, 0.0).astype(bf16)
            for part in range(count)
        ],
        1,
    )


def combine_kernel(place_ref, values_ref, out_ref, *, count, capacity):
    chosen = picks(place_ref, count, capacity)
    out_ref[...] = dot(chosen, values_ref[...]).astype(bf16)


def combine(places, values, capacity, block):
    tokens = places.shape[0]
    slots, width = values.shape
    return pl.pallas_call(
        functools.partial(combine_kernel, count=slots // capacity, capacity=capacity),
        grid=(tokens // block,),
        in_specs=[
            pl.BlockSpec((block, LANES), lambda i: (i, 0)),
            pl.BlockSpec((slots, width), lambda i: (0, 0)),
        ],
        out_specs=pl.BlockSpec((block, width), lambda i: (i, 0)),
        out_shape=jax.ShapeDtypeStruct((tokens, width), bf16),
        compiler_params=BIG,
        name="combine_rows",
    )(places, values)


def combine_add_kernel(own_ref, place_ref, values_ref, add_ref, out_ref, *, count, capacity):
    chosen = picks(place_ref, count, capacity)
    factor = jnp.where(pl.program_id(0) == own_ref[0], 1.0, 0.0)
    total = dot(chosen, values_ref[...]) + add_ref[...] * factor
    parts, _, width = out_ref.shape
    for part in range(parts):
        out_ref[part] = total[:, part * width : (part + 1) * width].astype(bf16)


def combine_add(own, places, values, addition, capacity, parts):
    tokens = places.shape[0]
    slots, width = values.shape
    block = addition.shape[0]
    return pl.pallas_call(
        functools.partial(combine_add_kernel, count=slots // capacity, capacity=capacity),
        grid=(tokens // block,),
        in_specs=[
            pl.BlockSpec(memory_space=pltpu.SMEM),
            pl.BlockSpec((block, LANES), lambda i: (i, 0)),
            pl.BlockSpec((slots, width), lambda i: (0, 0)),
            pl.BlockSpec((block, width), lambda i: (0, 0)),
        ],
        out_specs=pl.BlockSpec((parts, block, width // parts), lambda i: (0, i, 0)),
        out_shape=jax.ShapeDtypeStruct((parts, tokens, width // parts), bf16),
        compiler_params=BIG,
        name="combine_rows_add",
    )(own, places, values, addition)


def expert_kernel(
    slot_ref, grad_ref, up_ref, down_ref, router_ref, pick_ref,
    out_ref, back_ref, grad_up_ref, grad_down_ref,
):
    step = pl.program_id(0)
    width = slot_ref.shape[1]
    hidden_cols = down_ref.shape[0]
    slots = slot_ref[...]
    grads = grad_ref[:, :width].astype(f32)
    member = grad_ref[:, width:].astype(f32) > 0.5
    logits = jnp.where(member, dot(slots, router_ref[...]), masked_score)
    top = jnp.max(logits, -1, keepdims=True)
    powers = jnp.where(member, jnp.exp(logits - top), 0.0)
    mass = jnp.sum(powers, -1, keepdims=True)
    pick = pick_ref[...]
    gate = jnp.sum(powers * pick[0:1, :], -1, keepdims=True) / jnp.maximum(mass, 1e-30)
    both = dot(slots, up_ref[...])
    gate_part, up_part = both[:, :hidden_cols], both[:, hidden_cols:]
    sigmoid = 1.0 / (1.0 + jnp.exp(-gate_part))
    silu = gate_part * sigmoid
    hidden = (silu * up_part).astype(bf16)
    result = dot(hidden, down_ref[...])
    out_ref[...] = (result * gate).astype(bf16)
    dots = jnp.sum(result * grads, -1, keepdims=True)
    dots_high = dots.astype(bf16).astype(f32)
    back_ref[:, width:] = (dots_high * pick[0:1, :] + (dots - dots_high) * pick[1:2, :]).astype(
        bf16
    )
    grad_expert = (grads * gate).astype(bf16)
    grad_hidden = dot_nt(grad_expert, down_ref[...])
    grad_pair = jnp.concatenate(
        [
            grad_hidden * up_part * sigmoid * (1.0 + gate_part * (1.0 - sigmoid)),
            grad_hidden * silu,
        ],
        1,
    ).astype(bf16)
    back_ref[:, :width] = dot_nt(grad_pair, up_ref[...]).astype(bf16)

    @pl.when(step == 0)
    def _():
        grad_up_ref[...] = jnp.zeros_like(grad_up_ref)
        grad_down_ref[...] = jnp.zeros_like(grad_down_ref)

    grad_up_ref[...] += dot_tn(slots, grad_pair)
    grad_down_ref[...] += dot_tn(hidden, grad_expert)


def run_expert(slots, grads, up, down, router, pick, block):
    rows, width = slots.shape
    rest = grads.shape[1]
    hidden_cols = down.shape[0]
    whole = lambda shape: pl.BlockSpec(shape, lambda i: (0, 0))
    return pl.pallas_call(
        expert_kernel,
        grid=(rows // block,),
        in_specs=[
            pl.BlockSpec((block, width), lambda i: (i, 0)),
            pl.BlockSpec((block, rest), lambda i: (i, 0)),
            whole(up.shape),
            whole(down.shape),
            whole(router.shape),
            whole(pick.shape),
        ],
        out_specs=[
            pl.BlockSpec((block, width), lambda i: (i, 0)),
            pl.BlockSpec((block, rest), lambda i: (i, 0)),
            whole((width, 2 * hidden_cols)),
            whole((hidden_cols, width)),
        ],
        out_shape=[
            jax.ShapeDtypeStruct((rows, width), bf16),
            jax.ShapeDtypeStruct((rows, rest), bf16),
            jax.ShapeDtypeStruct((width, 2 * hidden_cols), f32),
            jax.ShapeDtypeStruct((hidden_cols, width), f32),
        ],
        compiler_params=BIG,
        name="expert_pass",
    )(slots, grads, up, down, router, pick)


def norm_back(grad, values, inv_rms, gain):
    scaled = grad * gain
    inner = jnp.mean(scaled * values, -1, keepdims=True)
    grad_gain = jnp.sum(grad * values * inv_rms, 0)
    return (inv_rms * scaled - values * inv_rms * inv_rms * inv_rms * inner, grad_gain)


def inverse_rms(values):
    return lax.rsqrt(jnp.mean(values * values, -1, keepdims=True) + epsilon)


def running_count(member):
    tokens, cols = member.shape
    chunk = LANES
    parts = member.reshape(tokens // chunk, chunk, cols)
    lower = jnp.tril(jnp.ones((chunk, chunk), f32))
    inside = jnp.einsum("ij,bjc->bic", lower, parts, preferred_element_type=f32)
    sums = jnp.sum(parts, 1)
    blocks = tokens // chunk
    before = jnp.sum(
        jnp.where(
            jnp.arange(blocks)[:, None, None] > jnp.arange(blocks)[None, :, None],
            sums[None, :, :],
            0.0,
        ),
        1,
    )
    return (inside + before[:, None, :]).reshape(tokens, cols).astype(jnp.int32)


def per_device(
    hidden_in,
    norm1_gain,
    query_weight,
    key_weight,
    value_weight,
    output_weight,
    norm2_gain,
    router_weight,
    gate_weight,
    up_weight,
    down_weight,
    segment_ids,
    expert_ids,
    grad_out,
):
    dp_count = lax.axis_size("dp")
    row_count = lax.axis_size("row")
    col_count = lax.axis_size("col")
    dp_at, row_at, col_at = (lax.axis_index(name) for name in ("dp", "row", "col"))
    cell = row_at * col_count + col_at
    cells = row_count * col_count
    local_rows, local_width = hidden_in.shape
    group, chosen = expert_ids.shape
    width = local_width * row_count
    experts = gate_weight.shape[0]
    hidden_part = gate_weight.shape[2]
    hidden_cols = hidden_part * col_count
    capacity = group * chosen * 5 // (4 * experts)
    sequences, seq_len = segment_ids.shape
    own_rows = seq_len // col_count
    query_cols, key_cols = query_weight.shape[1], key_weight.shape[1]
    kv_heads = key_cols // HEAD_DIM
    block = seq_len // 2
    spread = experts // cells
    copies = dp_count // spread
    per_dp = experts // dp_count
    assert sequences == row_count and spread * cells == experts and copies * spread == dp_count
    spread_at = dp_at % spread
    if copies == 1:
        near, far = None, None
    else:
        near = [[i * spread + j for j in range(spread)] for i in range(copies)]
        far = [[i * spread + j for i in range(copies)] for j in range(spread)]

    def exchange(rows):
        return lax.all_to_all(rows, "dp", 0, 0, axis_index_groups=near, tiled=True)

    def by_cell(array):
        lead = array.shape[:-1]
        split = array.reshape(lead + (copies, spread, per_dp))
        return jnp.swapaxes(split, -3, -2).reshape(lead + (spread, cells))

    qkv_own = jnp.concatenate([query_weight, key_weight, value_weight], 1)
    qkv_weight = lax.all_gather(qkv_own, "row", axis=0, tiled=True)
    columns = lax.all_gather(hidden_in, "col", axis=0, tiled=True)
    tokens_in = lax.all_to_all(columns, "row", 0, 1, tiled=True)
    gains = lax.all_gather(jnp.stack([norm1_gain, norm2_gain]), "row", axis=1, tiled=True)
    gain_one, gain_two = gains[0][None, :], gains[1][None, :]
    out_weight = lax.all_gather(output_weight, "row", axis=1, tiled=True)
    router = lax.all_gather(router_weight, "row", axis=0, tiled=True)
    router_pad = jnp.pad(router, ((0, 0), (0, LANES - experts)))
    grad_stack = lax.all_gather(grad_out, ("row", "col"), axis=0, tiled=True).reshape(
        row_count, group, local_width
    )

    def own_share(weight):
        split = weight.reshape((copies, spread, per_dp) + weight.shape[1:])
        return lax.dynamic_index_in_dim(split, spread_at, 1, keepdims=False).reshape(
            (cells,) + weight.shape[1:]
        )

    shares = jnp.concatenate(
        [own_share(gate_weight), own_share(up_weight), jnp.swapaxes(own_share(down_weight), 1, 2)],
        2,
    ).reshape(cells * local_width, 3 * hidden_part)
    got = lax.all_to_all(shares, ("row", "col"), 0, 0, tiled=True).reshape(
        row_count, col_count, local_width, 3, hidden_part
    )
    pair_weight = (
        got[:, :, :, :2, :].transpose(0, 2, 3, 1, 4).reshape(width, 2 * hidden_cols)
    )
    down_full = got[:, :, :, 2, :].transpose(1, 3, 0, 2).reshape(hidden_cols, width)

    member = jnp.any(
        expert_ids[:, :, None] == jnp.arange(experts, dtype=jnp.int32)[None, None, :], 1
    )
    mine = lax.dynamic_index_in_dim(
        by_cell(member.astype(f32)), cell, 2, keepdims=False
    )
    places = jnp.where(mine > 0.5, running_count(mine) - 1, -1)
    place_rows = places.T.reshape(spread, 1, group)
    place_cols = jnp.pad(places, ((0, 0), (0, LANES - spread)), constant_values=-1)
    member_pad = jnp.pad(member.astype(bf16), ((0, 0), (0, LANES - experts)))
    my_expert = ((cell // per_dp) * spread + spread_at) * per_dp + cell % per_dp
    lane = jnp.arange(LANES)[None, :]
    pick = jnp.concatenate(
        [
            (lane == my_expert).astype(f32),
            (lane == experts + my_expert).astype(f32),
            jnp.zeros((6, LANES), f32),
        ],
        0,
    )
    grad_slots = exchange(
        dispatch(place_rows, [grad_stack, member_pad[None]], capacity).reshape(
            spread * capacity, width + LANES
        )
    )

    tables = rope_tables(seq_len)
    segments = lax.dynamic_index_in_dim(segment_ids, row_at, 0, keepdims=True)
    seg_col = segments.reshape(seq_len, 1)
    residual = tokens_in.astype(f32)
    inv_one = inverse_rms(residual)
    normed_one = (residual * inv_one * gain_one).astype(bf16)
    raw = dot(normed_one, qkv_weight)
    query_low, key_low, value_low, heads, log_sums = attend_forward(
        raw, tables, seg_col, segments, kv_heads, block
    )
    attended = lax.psum_scatter(
        dot(heads, out_weight).astype(bf16), "col", scatter_dimension=0, tiled=True
    )
    own_start = col_at * own_rows
    middle = lax.dynamic_slice_in_dim(residual, own_start, own_rows, 0) + attended.astype(f32)
    inv_two = inverse_rms(middle)
    normed_two = (middle * inv_two * gain_two).astype(bf16)

    tokens_two = lax.all_gather(normed_two, ("row", "col"), axis=0, tiled=True)
    slots = exchange(
        dispatch(place_rows, [tokens_two[None]], capacity).reshape(spread * capacity, width)
    )
    results, back, grad_pair_w, grad_down_w = run_expert(
        slots, grad_slots, pair_weight, down_full, router_pad, pick, 256
    )
    back_rows = combine(place_cols, exchange(back), capacity, own_rows)
    grad_own = lax.psum_scatter(back_rows, ("row", "col"), scatter_dimension=0, tiled=True).astype(
        f32
    )
    mixed_rows = combine_add(
        cell.reshape(1), place_cols, exchange(results), middle, capacity, row_count
    )
    mixed_out = lax.psum_scatter(
        mixed_rows.reshape(cells * local_rows, local_width),
        ("row", "col"),
        scatter_dimension=0,
        tiled=True,
    )

    pair_split = grad_pair_w.reshape(row_count, local_width, 2, col_count, hidden_part)
    down_split = grad_down_w.reshape(col_count, hidden_part, row_count, local_width)
    grad_shares = jnp.concatenate(
        [
            pair_split.transpose(0, 3, 1, 2, 4).reshape(cells, local_width, 2 * hidden_part),
            down_split.transpose(2, 0, 3, 1).reshape(cells, local_width, hidden_part),
        ],
        2,
    ).astype(bf16)
    grad_got = lax.all_to_all(
        grad_shares.reshape(cells * local_width, 3 * hidden_part), ("row", "col"), 0, 0, tiled=True
    )
    if copies > 1:
        grad_got = lax.psum_scatter(
            grad_got, "dp", scatter_dimension=0, axis_index_groups=far, tiled=True
        )
    grad_got = grad_got.reshape(per_dp, local_width, 3, hidden_part).astype(f32)
    grad_gate, grad_up = grad_got[:, :, 0], grad_got[:, :, 1]
    grad_down = jnp.swapaxes(grad_got[:, :, 2], 1, 2)

    own_member = lax.dynamic_slice_in_dim(member, cell * own_rows, own_rows, 0)
    logits = jnp.where(own_member, dot(normed_two, router), masked_score)
    powers = jnp.where(own_member, jnp.exp(logits - jnp.max(logits, -1, keepdims=True)), 0.0)
    gates = powers / jnp.sum(powers, -1, keepdims=True)
    extra = grad_own[:, width:]
    grad_gates = extra[:, :experts] + extra[:, experts : 2 * experts]
    grad_logits = (
        gates * (grad_gates - jnp.sum(gates * grad_gates, -1, keepdims=True))
    ).astype(bf16)
    grad_router = dot_tn(normed_two, grad_logits)
    grad_two = grad_own[:, :width] + dot_nt(grad_logits, router)
    grad_norm, grad_gain_two = norm_back(grad_two, middle, inv_two, gain_two)
    own_grad = (
        lax.dynamic_slice_in_dim(grad_stack, cell * own_rows, own_rows, 1)
        .transpose(1, 0, 2)
        .reshape(own_rows, width)
    )
    grad_middle = own_grad.astype(f32) + grad_norm

    grad_mid = lax.all_gather(grad_middle.astype(bf16), "col", axis=0, tiled=True)
    grad_out_w = dot_tn(heads, grad_mid).astype(bf16)
    grad_heads = dot_nt(grad_mid, out_weight).astype(bf16)
    grad_qkv = jnp.concatenate(
        attend_backward(
            query_low, key_low, value_low, log_sums, grad_heads, tables, seg_col, segments, block
        ),
        1,
    )
    grad_qkv_w = dot_tn(normed_one, grad_qkv).astype(bf16)
    grad_one = dot_nt(grad_qkv, qkv_weight)
    grad_part, grad_gain_one = norm_back(grad_one, residual, inv_one, gain_one)
    at_own = lax.dynamic_slice_in_dim(grad_part, own_start, own_rows, 0) + grad_middle
    grad_part = lax.dynamic_update_slice_in_dim(grad_part, at_own, own_start, 0)
    grad_cols = lax.all_to_all(grad_part.astype(bf16), "row", 1, 0, tiled=True)
    grad_in = lax.psum_scatter(grad_cols, "col", scatter_dimension=0, tiled=True).astype(f32)

    qkv_sum = lax.psum(
        lax.psum_scatter(grad_qkv_w, "row", scatter_dimension=0, tiled=True), "dp"
    ).astype(f32)
    out_sum = lax.psum(
        lax.psum_scatter(grad_out_w, "row", scatter_dimension=1, tiled=True), "dp"
    ).astype(f32)
    small = lax.psum(
        (grad_gain_one, grad_gain_two, grad_router), ("dp", "row", "col")
    )
    mine_of = lambda array: lax.dynamic_slice_in_dim(array, row_at * local_width, local_width, 0)
    return (
        mixed_out,
        grad_in,
        mine_of(small[0]),
        qkv_sum[:, :query_cols],
        qkv_sum[:, query_cols : query_cols + key_cols],
        qkv_sum[:, query_cols + key_cols :],
        out_sum,
        mine_of(small[1]),
        mine_of(small[2]),
        grad_gate,
        grad_up,
        grad_down,
    )


def solution(mesh):
    return jax.shard_map(
        per_device,
        mesh=mesh,
        in_specs=(
            P(("dp", "col"), "row"),
            P("row"),
            P("row", "col"),
            P("row", "col"),
            P("row", "col"),
            P("col", "row"),
            P("row"),
            P("row", None),
            P(None, "row", "col"),
            P(None, "row", "col"),
            P(None, "col", "row"),
            P("dp", None),
            P("dp", None),
            P(("dp", "col"), "row"),
        ),
        out_specs=(
            P(("dp", "col"), "row"),
            P(("dp", "col"), "row"),
            P("row"),
            P("row", "col"),
            P("row", "col"),
            P("row", "col"),
            P("col", "row"),
            P("row"),
            P("row", None),
            P("dp", "row", "col"),
            P("dp", "row", "col"),
            P("dp", "col", "row"),
        ),
        check_vma=False,
    )
```

```python
import functools

import jax
import jax.numpy as jnp
from jax import lax
from jax.experimental import pallas as pl
from jax.experimental.pallas import tpu as pltpu
from jax.sharding import PartitionSpec as P

HEAD_DIM = 64
LANES = 128

epsilon = 1e-06
rope_base = 10000.0
masked_score = -1e30

f32 = jnp.float32
bf16 = jnp.bfloat16

BIG = pltpu.CompilerParams(vmem_limit_bytes=56 * 1024 * 1024)


def dot(left, right):
    return lax.dot_general(left, right, (((1,), (0,)), ((), ())), preferred_element_type=f32)


def dot_nt(left, right):
    return lax.dot_general(left, right, (((1,), (1,)), ((), ())), preferred_element_type=f32)


def dot_tn(left, right):
    return lax.dot_general(left, right, (((0,), (0,)), ((), ())), preferred_element_type=f32)


def rope_tables(seq_len):
    midpoint = HEAD_DIM // 2
    frequency = rope_base ** (-2.0 * jnp.arange(midpoint, dtype=f32) / HEAD_DIM)
    angles = jnp.arange(seq_len, dtype=f32)[:, None] * frequency[None, :]
    cosines, sines = jnp.cos(angles), jnp.sin(angles)
    return (
        jnp.tile(cosines, (1, LANES // midpoint)),
        jnp.tile(jnp.concatenate([-sines, sines], 1), (1, LANES // HEAD_DIM)),
    )


def partner(tile):
    lane = lax.broadcasted_iota(jnp.int32, tile.shape, 1)
    half = HEAD_DIM // 2
    return jnp.where(
        (lane % HEAD_DIM) < half,
        pltpu.roll(tile, LANES - half, 1),
        pltpu.roll(tile, half, 1),
    )


def spread_pair(tile):
    tile = tile.astype(f32)
    lane = lax.broadcasted_iota(jnp.int32, tile.shape, 1)
    swapped = pltpu.roll(tile, HEAD_DIM, 1)
    low = lane < HEAD_DIM
    return (
        jnp.where(low, tile, swapped).astype(bf16),
        jnp.where(low, swapped, tile).astype(bf16),
    )


def split_heads(tile):
    lane = lax.broadcasted_iota(jnp.int32, tile.shape, 1)
    low = lane < HEAD_DIM
    zero = jnp.zeros_like(tile)
    return jnp.where(low, tile, zero), jnp.where(low, zero, tile)


def block_mask(seg_col, seg_row, start, rows, keys):
    row = lax.broadcasted_iota(jnp.int32, (rows, keys), 0) + start
    key = lax.broadcasted_iota(jnp.int32, (rows, keys), 1)
    return (key <= row) & (seg_col[start : start + rows, :] == seg_row[:, :keys])


def attend_kernel(
    query_in, key_in, value_in, cos_ref, sin_ref, col_ref, row_ref,
    query_out, key_out, value_out, heads_out, sums_out, *, block
):
    seq_len = query_in.shape[0]
    cosines, sines = cos_ref[...], sin_ref[...]
    key = key_in[...]
    key_low = (key * cosines + partner(key) * sines).astype(bf16)
    key_out[...] = key_low
    value_low = value_in[...].astype(bf16)
    value_out[...] = value_low
    keys, values = spread_pair(key_low), spread_pair(value_low)
    lane = lax.broadcasted_iota(jnp.int32, (block, LANES), 1)
    scale = 1.0 / HEAD_DIM
    for group in range(2):
        cols = slice(group * LANES, (group + 1) * LANES)
        query = query_in[:, cols]
        query_low = (query * cosines + partner(query) * sines).astype(bf16)
        query_out[:, cols] = query_low
        parts = split_heads(query_low)
        value_parts = split_heads(values[group])
        for start in range(0, seq_len, block):
            reach = start + block
            mask = block_mask(col_ref[...], row_ref[...], start, block, reach)
            total = jnp.zeros((block, LANES), f32)
            for head in range(2):
                scores = dot_nt(parts[head][start:reach], keys[group][:reach]) * scale
                scores = jnp.where(mask, scores, masked_score)
                top = jnp.max(scores, -1, keepdims=True)
                powers = jnp.exp(scores - top)
                mass = jnp.sum(powers, -1, keepdims=True)
                attention = (powers / mass).astype(bf16)
                total += dot(attention, value_parts[head][:reach])
                place = group * 2 + head
                sums = jnp.broadcast_to(top + jnp.log(mass), (block, LANES))
                if place == 0:
                    sums_out[start:reach, :] = sums
                else:
                    sums_out[start:reach, :] = jnp.where(
                        lane == place, sums, sums_out[start:reach, :]
                    )
            heads_out[start:reach, cols] = total.astype(bf16)


def attend_forward(raw, tables, seg_col, seg_row, kv_heads, block):
    seq_len = raw.shape[0]
    pairs = kv_heads // 2
    width = pairs * LANES
    spec = lambda cols, at: pl.BlockSpec((seq_len, cols), at)
    return pl.pallas_call(
        functools.partial(attend_kernel, block=block),
        grid=(pairs,),
        in_specs=[
            spec(2 * LANES, lambda i: (0, i)),
            spec(LANES, lambda i: (0, 2 * pairs + i)),
            spec(LANES, lambda i: (0, 3 * pairs + i)),
            spec(LANES, lambda i: (0, 0)),
            spec(LANES, lambda i: (0, 0)),
            pl.BlockSpec((seq_len, 1), lambda i: (0, 0)),
            pl.BlockSpec((1, seq_len), lambda i: (0, 0)),
        ],
        out_specs=[
            spec(2 * LANES, lambda i: (0, i)),
            spec(LANES, lambda i: (0, i)),
            spec(LANES, lambda i: (0, i)),
            spec(2 * LANES, lambda i: (0, i)),
            spec(LANES, lambda i: (0, i)),
        ],
        out_shape=[
            jax.ShapeDtypeStruct((seq_len, 2 * width), bf16),
            jax.ShapeDtypeStruct((seq_len, width), bf16),
            jax.ShapeDtypeStruct((seq_len, width), bf16),
            jax.ShapeDtypeStruct((seq_len, 2 * width), bf16),
            jax.ShapeDtypeStruct((seq_len, width), f32),
        ],
        compiler_params=BIG,
        name="attend_forward",
    )(raw, raw, raw, *tables, seg_col, seg_row)


def attend_back_kernel(
    query_in, key_in, value_in, sums_in, grad_in, cos_ref, sin_ref, col_ref, row_ref,
    query_out, key_out, value_out, key_sum, value_sum, *, block
):
    seq_len = query_in.shape[0]
    keys, values = spread_pair(key_in[...]), spread_pair(value_in[...])
    lane = lax.broadcasted_iota(jnp.int32, (seq_len, LANES), 1)
    low = lane < HEAD_DIM
    scale = 1.0 / HEAD_DIM
    folded = []
    for group in range(2):
        cols = slice(group * LANES, (group + 1) * LANES)
        query_parts = split_heads(query_in[:, cols])
        grad_parts = split_heads(grad_in[:, cols])
        key_parts = split_heads(keys[group])
        key_sum[...] = jnp.zeros_like(key_sum)
        value_sum[...] = jnp.zeros_like(value_sum)
        for start in range(0, seq_len, block):
            reach = start + block
            rows = slice(start, reach)
            mask = block_mask(col_ref[...], row_ref[...], start, block, reach)
            total = jnp.zeros((block, LANES), f32)
            for head in range(2):
                place = group * 2 + head
                query, grad = query_parts[head][rows], grad_parts[head][rows]
                scores = dot_nt(query, keys[group][:reach]) * scale
                powers = jnp.exp(scores - sums_in[rows, place : place + 1])
                attention = jnp.where(mask, powers, 0.0)
                value_sum[:reach, :] += dot_tn(attention.astype(bf16), grad)
                grad_probs = dot_nt(grad, values[group][:reach])
                inner = jnp.sum(grad_probs * attention, -1, keepdims=True)
                grad_scores = (attention * (grad_probs - inner) * scale).astype(bf16)
                key_sum[:reach, :] += dot_tn(grad_scores, query)
                total += dot(grad_scores, key_parts[head][:reach])
            cosines, sines = cos_ref[rows, :], sin_ref[rows, :]
            query_out[rows, cols] = (total * cosines - partner(total) * sines).astype(bf16)
        grad_key, grad_value = key_sum[...], value_sum[...]
        folded.append(
            (
                grad_key + pltpu.roll(grad_key, HEAD_DIM, 1),
                grad_value + pltpu.roll(grad_value, HEAD_DIM, 1),
            )
        )
    grad_key = jnp.where(low, folded[0][0], folded[1][0])
    grad_value = jnp.where(low, folded[0][1], folded[1][1])
    key_out[...] = (grad_key * cos_ref[...] - partner(grad_key) * sin_ref[...]).astype(bf16)
    value_out[...] = grad_value.astype(bf16)


def attend_backward(query, key, value, sums, grad, tables, seg_col, seg_row, block):
    seq_len = query.shape[0]
    width = key.shape[1]
    pairs = width // LANES
    spec = lambda cols, at: pl.BlockSpec((seq_len, cols), at)
    here = lambda i: (0, i)
    first = lambda i: (0, 0)
    return pl.pallas_call(
        functools.partial(attend_back_kernel, block=block),
        grid=(pairs,),
        in_specs=[
            spec(2 * LANES, here),
            spec(LANES, here),
            spec(LANES, here),
            spec(LANES, here),
            spec(2 * LANES, here),
            spec(LANES, first),
            spec(LANES, first),
            pl.BlockSpec((seq_len, 1), first),
            pl.BlockSpec((1, seq_len), first),
        ],
        out_specs=[spec(2 * LANES, here), spec(LANES, here), spec(LANES, here)],
        out_shape=[
            jax.ShapeDtypeStruct((seq_len, 2 * width), bf16),
            jax.ShapeDtypeStruct((seq_len, width), bf16),
            jax.ShapeDtypeStruct((seq_len, width), bf16),
        ],
        scratch_shapes=[pltpu.VMEM((seq_len, LANES), f32), pltpu.VMEM((seq_len, LANES), f32)],
        compiler_params=BIG,
        name="attend_backward",
    )(query, key, value, sums, grad, *tables, seg_col, seg_row)


def place_rows_of(place_ref, starts_ref, which, tokens, window, capacity):
    start = starts_ref[which]
    start = pl.multiple_of(jnp.minimum(start - start % 16, capacity - window), 16)
    slots = lax.broadcasted_iota(jnp.int32, (window, tokens), 0) + start
    return start, jnp.where(slots == place_ref, 1.0, 0.0).astype(bf16)


def store_at(step, refs, value):
    for index, ref in enumerate(refs):

        @pl.when(step == index)
        def _():
            ref[...] = value


def dispatch_two_kernel(starts_ref, place_ref, *refs, count):
    blocks, out_refs, total = refs[: -1 - count], refs[-1 - count : -1], refs[-1]
    tokens = blocks[0].shape[0]
    capacity = total.shape[0]
    window = tokens + 16
    expert = pl.program_id(0)
    total[...] = jnp.zeros_like(total)
    for index, block in enumerate(blocks):
        start, chosen = place_rows_of(
            place_ref[0, :, index * tokens : (index + 1) * tokens],
            starts_ref,
            expert * len(blocks) + index,
            tokens,
            window,
            capacity,
        )
        total[pl.ds(start, window), :] += dot(chosen, block[...])
    store_at(expert, out_refs, total[...].astype(bf16))


def dispatch_grads_kernel(starts_ref, place_ref, stack_ref, member_ref, *refs, block):
    *out_refs, total = refs
    parts, tokens, width = stack_ref.shape
    capacity = total.shape[0]
    window = block + 16
    expert = pl.program_id(0)
    total[...] = jnp.zeros_like(total)
    steps = tokens // block
    for step in range(steps):
        rows = slice(step * block, (step + 1) * block)
        start, chosen = place_rows_of(
            place_ref[0, :, rows], starts_ref, expert * steps + step, block, window, capacity
        )
        values = jnp.concatenate(
            [stack_ref[part, rows, :] for part in range(parts)] + [member_ref[rows, :]], 1
        )
        total[pl.ds(start, window), :] += dot(chosen, values)
    store_at(expert, out_refs, total[...].astype(bf16))


def dispatch(kernel, name, starts, places, arrays, capacity, width):
    count, _, tokens = places.shape
    whole = lambda array: pl.BlockSpec(array.shape, lambda i: (0,) * array.ndim)
    return pl.pallas_call(
        kernel,
        grid=(count,),
        in_specs=[
            pl.BlockSpec(memory_space=pltpu.SMEM),
            pl.BlockSpec((1, 1, tokens), lambda i: (i, 0, 0)),
        ]
        + [whole(array) for array in arrays],
        out_specs=[pl.BlockSpec((capacity, width), lambda i: (0, 0))] * count,
        out_shape=[jax.ShapeDtypeStruct((capacity, width), bf16)] * count,
        scratch_shapes=[pltpu.VMEM((capacity, width), f32)],
        compiler_params=BIG,
        name=name,
    )(starts, places, *arrays)


def dispatch_two(starts, places, blocks, capacity):
    count = places.shape[0]
    kernel = functools.partial(dispatch_two_kernel, count=count)
    width = blocks[0].shape[1]
    return dispatch(kernel, "dispatch_tokens", starts, places, blocks, capacity, width)


def dispatch_grads(starts, places, stack, members, capacity, block):
    kernel = functools.partial(dispatch_grads_kernel, block=block)
    width = stack.shape[0] * stack.shape[2] + LANES
    return dispatch(
        kernel, "dispatch_grads", starts, places, [stack, members], capacity, width
    )


def gather_back(starts_ref, place_ref, value_refs, which, capacity):
    tokens = place_ref.shape[0]
    window = 2 * tokens
    count = len(value_refs)
    total = None
    for expert, values_ref in enumerate(value_refs):
        start = starts_ref[which * count + expert]
        start = pl.multiple_of(jnp.minimum(start - start % 16, capacity - window), 16)
        slots = lax.broadcasted_iota(jnp.int32, (tokens, window), 1) + start
        chosen = jnp.where(slots == place_ref[:, expert : expert + 1], 1.0, 0.0).astype(bf16)
        term = dot(chosen, values_ref[pl.ds(start, window), :])
        total = term if total is None else total + term
    return total


def combine_kernel(starts_ref, place_ref, *refs, capacity):
    *value_refs, own_ref, away_ref = refs
    step = pl.program_id(0)
    half = pl.num_programs(0) // 2
    pieces = place_ref.shape[0] // LANES
    for piece in range(pieces):
        rows = slice(piece * LANES, (piece + 1) * LANES)
        total = gather_back(
            starts_ref, place_ref[rows, :], value_refs, step * pieces + piece, capacity
        ).astype(bf16)

        @pl.when(step < half)
        def _():
            away_ref[0, rows, :] = total

        @pl.when(step >= half)
        def _():
            own_ref[0, rows, :] = total


def combine(starts, places, values, block):
    tokens = places.shape[0]
    capacity, width = values[0].shape
    half = tokens // block // 2
    out = jax.ShapeDtypeStruct((half, block, width), bf16)
    return pl.pallas_call(
        functools.partial(combine_kernel, capacity=capacity),
        grid=(2 * half,),
        in_specs=[
            pl.BlockSpec(memory_space=pltpu.SMEM),
            pl.BlockSpec((block, LANES), lambda i: (i, 0)),
        ]
        + [pl.BlockSpec((capacity, width), lambda i: (0, 0)) for _ in values],
        out_specs=[
            pl.BlockSpec((1, block, width), lambda i: (jnp.maximum(i - half, 0), 0, 0)),
            pl.BlockSpec((1, block, width), lambda i: (jnp.minimum(i, half - 1), 0, 0)),
        ],
        out_shape=[out, out],
        compiler_params=BIG,
        name="combine_rows",
    )(starts, places, *values)


def combine_add_kernel(own_ref, starts_ref, place_ref, add_ref, *refs, capacity):
    *value_refs, out_ref = refs
    step = pl.program_id(0)
    factor = jnp.where(step == own_ref[0], 1.0, 0.0)
    parts, block, width = out_ref.shape
    pieces = block // LANES
    for piece in range(pieces):
        rows = slice(piece * LANES, (piece + 1) * LANES)
        total = gather_back(
            starts_ref, place_ref[rows, :], value_refs, step * pieces + piece, capacity
        )
        total += add_ref[rows, :] * factor
        for part in range(parts):
            out_ref[part, rows, :] = total[:, part * width : (part + 1) * width].astype(bf16)


def combine_add(own, starts, places, values, addition, parts):
    tokens = places.shape[0]
    capacity, width = values[0].shape
    block = addition.shape[0]
    return pl.pallas_call(
        functools.partial(combine_add_kernel, capacity=capacity),
        grid=(tokens // block,),
        in_specs=[
            pl.BlockSpec(memory_space=pltpu.SMEM),
            pl.BlockSpec(memory_space=pltpu.SMEM),
            pl.BlockSpec((block, LANES), lambda i: (i, 0)),
            pl.BlockSpec((block, width), lambda i: (0, 0)),
        ]
        + [pl.BlockSpec((capacity, width), lambda i: (0, 0)) for _ in values],
        out_specs=pl.BlockSpec((parts, block, width // parts), lambda i: (0, i, 0)),
        out_shape=jax.ShapeDtypeStruct((parts, tokens, width // parts), bf16),
        compiler_params=BIG,
        name="combine_rows_add",
    )(own, starts, places, addition, *values)


def expert_kernel(
    weight_ref, router_ref, pick_ref, *refs, groups, row_count, col_count
):
    slot_refs, grad_refs = refs[:groups], refs[groups : 2 * groups]
    out_refs, back_a_refs, back_b_refs = (
        refs[at * groups : (at + 1) * groups] for at in (2, 3, 4)
    )
    grad_weight_ref, up_ref, down_ref, grad_up_ref, grad_down_ref, slot_ref, grad_ref = refs[
        5 * groups :
    ]
    step = pl.program_id(0) * pl.num_programs(1) + pl.program_id(1)
    last = pl.num_programs(0) * pl.num_programs(1) - 1
    width = slot_ref.shape[1]
    split = back_b_refs[0].shape[1]
    for group in range(groups):

        @pl.when(pl.program_id(0) == group)
        def _():
            slot_ref[...] = slot_refs[group][...]
            grad_ref[...] = grad_refs[group][...]

    hidden_cols = down_ref.shape[0]
    part = weight_ref.shape[2]

    def blocks():
        for row in range(row_count):
            for col in range(col_count):
                rows = slice(row * part, (row + 1) * part)
                cols = slice(col * part, (col + 1) * part)
                above = slice(hidden_cols + col * part, hidden_cols + (col + 1) * part)
                yield row * col_count + col, rows, cols, above

    @pl.when(step == 0)
    def _():
        for cell, rows, cols, above in blocks():
            up_ref[rows, cols] = weight_ref[cell, :part, :]
            up_ref[rows, above] = weight_ref[cell, part : 2 * part, :]
            down_ref[cols, rows] = weight_ref[cell, 2 * part :, :]
        grad_up_ref[...] = jnp.zeros_like(grad_up_ref)
        grad_down_ref[...] = jnp.zeros_like(grad_down_ref)

    slots = slot_ref[...]
    grads = grad_ref[:, :width].astype(f32)
    member = grad_ref[:, width:].astype(f32) > 0.5
    logits = jnp.where(member, dot(slots, router_ref[...]), masked_score)
    top = jnp.max(logits, -1, keepdims=True)
    powers = jnp.where(member, jnp.exp(logits - top), 0.0)
    mass = jnp.sum(powers, -1, keepdims=True)
    pick = pick_ref[...]
    gate = jnp.sum(powers * pick[0:1, :], -1, keepdims=True) / jnp.maximum(mass, 1e-30)
    both = dot(slots, up_ref[...])
    gate_part, up_part = both[:, :hidden_cols], both[:, hidden_cols:]
    sigmoid = 1.0 / (1.0 + jnp.exp(-gate_part))
    silu = gate_part * sigmoid
    hidden = (silu * up_part).astype(bf16)
    result = dot(hidden, down_ref[...])
    scaled = (result * gate).astype(bf16)
    dots = jnp.sum(result * grads, -1, keepdims=True)
    dots_high = dots.astype(bf16).astype(f32)
    dots_low = dots - dots_high
    split_dots = (dots_high * pick[0:1, :] + dots_low * pick[1:2, :]).astype(bf16)
    grad_expert = (grads * gate).astype(bf16)
    grad_hidden = dot_nt(grad_expert, down_ref[...])
    grad_pair = jnp.concatenate(
        [
            grad_hidden * up_part * sigmoid * (1.0 + gate_part * (1.0 - sigmoid)),
            grad_hidden * silu,
        ],
        1,
    ).astype(bf16)
    back = dot_nt(grad_pair, up_ref[...]).astype(bf16)
    for group in range(groups):

        @pl.when(pl.program_id(0) == group)
        def _():
            out_refs[group][...] = scaled
            back_a_refs[group][:, :LANES] = split_dots
            back_a_refs[group][:, LANES:] = back[:, : width - split]
            back_b_refs[group][...] = back[:, width - split :]

    grad_up_ref[...] += dot_tn(slots, grad_pair)
    grad_down_ref[...] += dot_tn(hidden, grad_expert)

    @pl.when(step == last)
    def _():
        for cell, rows, cols, above in blocks():
            grad_weight_ref[cell, :part, :] = grad_up_ref[rows, cols].astype(bf16)
            grad_weight_ref[cell, part : 2 * part, :] = grad_up_ref[rows, above].astype(bf16)
            grad_weight_ref[cell, 2 * part :, :] = grad_down_ref[cols, rows].astype(bf16)


def run_expert(slots, grads, weights, router, pick, steps, row_count, col_count):
    groups = len(slots)
    capacity, width = slots[0].shape
    rest = grads[0].shape[1]
    half = width // 2
    block = capacity // steps
    hidden_cols = weights.shape[2] * col_count
    whole = lambda shape: pl.BlockSpec(shape, lambda i, j: (0,) * len(shape))

    def some(cols):
        def spec(group):
            return pl.BlockSpec(
                (block, cols),
                lambda i, j: (
                    jnp.where(i < group, 0, jnp.where(i > group, steps - 1, j)),
                    0,
                ),
            )

        return [spec(group) for group in range(groups)]

    shapes = lambda cols: [jax.ShapeDtypeStruct((capacity, cols), bf16)] * groups
    outs = pl.pallas_call(
        functools.partial(
            expert_kernel, groups=groups, row_count=row_count, col_count=col_count
        ),
        grid=(groups, steps),
        in_specs=[whole(weights.shape), whole(router.shape), whole(pick.shape)]
        + some(width)
        + some(rest),
        out_specs=some(width) + some(half + LANES) + some(half) + [whole(weights.shape)],
        out_shape=shapes(width)
        + shapes(half + LANES)
        + shapes(half)
        + [jax.ShapeDtypeStruct(weights.shape, bf16)],
        scratch_shapes=[
            pltpu.VMEM((width, 2 * hidden_cols), bf16),
            pltpu.VMEM((hidden_cols, width), bf16),
            pltpu.VMEM((width, 2 * hidden_cols), f32),
            pltpu.VMEM((hidden_cols, width), f32),
            pltpu.VMEM((block, width), bf16),
            pltpu.VMEM((block, rest), bf16),
        ],
        compiler_params=BIG,
        name="expert_pass",
    )(weights, router, pick, *slots, *grads)
    return (
        outs[:groups],
        outs[groups : 2 * groups],
        outs[2 * groups : 3 * groups],
        outs[3 * groups],
    )


def spread_kernel(block_ref, *out_refs):
    part = out_refs[0].shape[1]
    for index, out_ref in enumerate(out_refs):
        out_ref[0] = block_ref[0, index * part : (index + 1) * part, :].astype(f32)


def spread_blocks(blocks, count):
    cells, rows, cols = blocks.shape
    part = rows // count
    return pl.pallas_call(
        spread_kernel,
        grid=(cells,),
        in_specs=[pl.BlockSpec((1, rows, cols), lambda i: (i, 0, 0))],
        out_specs=[pl.BlockSpec((1, part, cols), lambda i: (i, 0, 0))] * count,
        out_shape=[jax.ShapeDtypeStruct((cells, part, cols), f32)] * count,
        compiler_params=BIG,
        name="spread_blocks",
    )(blocks)


def norm_back(grad, values, inv_rms, gain):
    scaled = grad * gain
    inner = jnp.mean(scaled * values, -1, keepdims=True)
    grad_gain = jnp.sum(grad * values * inv_rms, 0)
    return (inv_rms * scaled - values * inv_rms * inv_rms * inv_rms * inner, grad_gain)


def inverse_rms(values):
    return lax.rsqrt(jnp.mean(values * values, -1, keepdims=True) + epsilon)


def running_count(member):
    tokens, cols = member.shape
    chunk = LANES
    parts = member.reshape(tokens // chunk, chunk, cols)
    lower = jnp.tril(jnp.ones((chunk, chunk), f32))
    inside = jnp.einsum("ij,bjc->bic", lower, parts, preferred_element_type=f32)
    sums = jnp.sum(parts, 1)
    blocks = tokens // chunk
    before = jnp.sum(
        jnp.where(
            jnp.arange(blocks)[:, None, None] > jnp.arange(blocks)[None, :, None],
            sums[None, :, :],
            0.0,
        ),
        1,
    )
    return (inside + before[:, None, :]).reshape(tokens, cols).astype(jnp.int32)


def per_device(
    hidden_in,
    norm1_gain,
    query_weight,
    key_weight,
    value_weight,
    output_weight,
    norm2_gain,
    router_weight,
    gate_weight,
    up_weight,
    down_weight,
    segment_ids,
    expert_ids,
    grad_out,
):
    dp_count = lax.axis_size("dp")
    row_count = lax.axis_size("row")
    col_count = lax.axis_size("col")
    dp_at, row_at, col_at = (lax.axis_index(name) for name in ("dp", "row", "col"))
    cell = row_at * col_count + col_at
    cells = row_count * col_count
    local_rows, local_width = hidden_in.shape
    group, chosen = expert_ids.shape
    width = local_width * row_count
    experts = gate_weight.shape[0]
    hidden_part = gate_weight.shape[2]
    hidden_cols = hidden_part * col_count
    capacity = group * chosen * 5 // (4 * experts)
    sequences, seq_len = segment_ids.shape
    own_rows = seq_len // col_count
    query_cols, key_cols = query_weight.shape[1], key_weight.shape[1]
    kv_heads = key_cols // HEAD_DIM
    block = seq_len // 2
    spread = experts // cells
    copies = dp_count // spread
    per_dp = experts // dp_count
    assert sequences == row_count and spread * cells == experts and copies * spread == dp_count
    spread_at = dp_at % spread
    if copies == 1:
        far = None
    else:
        far = [[i * spread + j for i in range(copies)] for j in range(spread)]

    def exchange(arrays):
        return [over_dp(array, turn) for turn, array in enumerate(arrays)]

    def by_cell(array):
        lead = array.shape[:-1]
        split = array.reshape(lead + (copies, spread, per_dp))
        return jnp.swapaxes(split, -3, -2).reshape(lead + (spread, cells))

    per_col = sequences // col_count
    part_at = (row_at // col_count) * col_count + col_at
    sequence_of = lambda row: (row % col_count) * per_col + row // col_count
    block_of = lambda row, col: sequence_of(row) * col_count + col
    own_block = block_of(row_at, col_at)

    def rounds():
        for turn in range(row_count):
            there, back = [], []
            for row in range(row_count):
                for col in range(col_count):
                    part = (row - turn) % row_count
                    other = ((part // col_count) * col_count + col) * col_count + part % col_count
                    there.append((row * col_count + col, other))
                    back.append((other, row * col_count + col))
            yield turn, there, back

    def to_sequences(array):
        parts = array.reshape(per_col, seq_len, local_width)
        got = []
        for turn, there, _ in rounds():
            part = (row_at - turn) % row_count
            own = lax.dynamic_index_in_dim(parts, part // col_count, 0, keepdims=False)
            got.append(lax.ppermute(own, ("row", "col"), there))
        got = jnp.stack(got)
        return jnp.concatenate(
            [
                lax.dynamic_index_in_dim(got, (row - part_at) % row_count, 0, keepdims=False)
                for row in range(row_count)
            ],
            1,
        )

    def from_sequences(array):
        parts = array.reshape(seq_len, row_count, local_width).transpose(1, 0, 2)
        got = []
        for turn, _, back in rounds():
            own = lax.dynamic_index_in_dim(
                parts, (turn + part_at) % row_count, 0, keepdims=False
            )
            got.append(lax.ppermute(own, ("row", "col"), back).astype(f32))
        total = []
        for index in range(per_col):
            total.append(
                sum(
                    jnp.where(((row_at - turn) % row_count) // col_count == index, got[turn], 0.0)
                    for turn in range(row_count)
                )
            )
        return jnp.concatenate(total, 0)

    own_start = col_at * own_rows
    mirror = [(col, col_count - 1 - col) for col in range(col_count)]

    def sum_halves(array):
        parts = array.reshape(col_count, own_rows, array.shape[1])
        away = lax.dynamic_index_in_dim(parts, 1 - col_at, 0, keepdims=False).astype(bf16)
        own = lax.dynamic_index_in_dim(parts, col_at, 0, keepdims=False)
        return own + lax.ppermute(away, "col", mirror).astype(f32)

    def join_halves(array):
        other = lax.ppermute(array, "col", mirror)
        first = col_at == 0
        return jnp.concatenate(
            [jnp.where(first, array, other), jnp.where(first, other, array)], 0
        )

    def in_terms(array):
        terms = []
        for _ in range(3):
            terms.append(array.astype(bf16))
            array = array - terms[-1].astype(f32)
        return terms

    tokens_in = to_sequences(hidden_in)
    extras = jnp.concatenate(
        [router_weight, jnp.stack(in_terms(norm1_gain) + in_terms(norm2_gain), 1)], 1
    )
    def over_rows(array, turn):
        pairs = [(row, row ^ turn) for row in range(row_count)]
        return lax.ppermute(array, "row", pairs) if turn else array

    def over_dp(array, turn):
        pairs = [(at, at ^ turn) for at in range(dp_count)]
        return lax.ppermute(array, "dp", pairs) if turn else array

    def over_cells(array, turn):
        pairs = [(at, at ^ turn) for at in range(cells)]
        return lax.ppermute(array, ("row", "col"), pairs) if turn else array

    pick_from = lambda array, at: lax.dynamic_index_in_dim(array, at, 0, keepdims=False)

    def all_rows(array):
        share = local_width // spread
        own = lax.dynamic_slice_in_dim(array, spread_at * share, share, 0)
        rows = jnp.stack([over_rows(own, turn) for turn in range(row_count)])
        rows = jnp.stack([pick_from(rows, row_at ^ row) for row in range(row_count)])
        shares = jnp.stack([over_dp(rows, turn) for turn in range(spread)])
        ordered = jnp.stack([pick_from(shares, spread_at ^ at) for at in range(spread)], 1)
        return ordered.reshape(width, array.shape[1])

    qkv_cols = query_cols + 2 * key_cols
    first_weights = all_rows(
        jnp.concatenate(
            [
                query_weight,
                key_weight,
                value_weight,
                jnp.pad(extras, ((0, 0), (0, LANES - extras.shape[1]))),
            ],
            1,
        )
    )
    first_weights, grad_late = lax.optimization_barrier((first_weights, grad_out))
    grad_stack = lax.all_gather(grad_late, ("row", "col"), axis=0, tiled=True).reshape(
        row_count, group, local_width
    )

    qkv_weight = first_weights[:, :qkv_cols]
    extras = first_weights[:, qkv_cols:]
    out_weight = all_rows(output_weight.T)
    router_pad = jnp.where(jnp.arange(LANES)[None, :] < experts, extras, jnp.zeros((), bf16))
    router = extras[:, :experts]
    terms = extras[:, experts : experts + 6].astype(f32)
    gain_one = (terms[:, 0] + terms[:, 1] + terms[:, 2])[None, :]
    gain_two = (terms[:, 3] + terms[:, 4] + terms[:, 5])[None, :]
    def from_cells(array):
        rows = [over_rows(array, turn) for turn in range(row_count)]
        return [(block, lax.ppermute(block, "col", mirror)) for block in rows]

    member = jnp.any(
        expert_ids[:, :, None] == jnp.arange(experts, dtype=jnp.int32)[None, None, :], 1
    )
    mine = lax.dynamic_index_in_dim(
        by_cell(member.astype(f32)), cell, 2, keepdims=False
    )
    mine = jnp.concatenate(
        [lax.dynamic_slice_in_dim(mine, spread_at ^ turn, 1, 1) for turn in range(spread)], 1
    )
    places = jnp.where(mine > 0.5, running_count(mine) - 1, -1)
    first = running_count(mine) - mine.astype(jnp.int32)
    token_blocks = places.reshape(cells, own_rows, spread)
    first_blocks = first.reshape(cells, own_rows, spread)[:, ::LANES]
    pad_cols = lambda array: jnp.pad(
        array, ((0, 0), (0, LANES - spread)), constant_values=-1
    )
    arrival = [
        block_of(row_at ^ turn, col_at ^ side)
        for turn in range(row_count)
        for side in range(2)
    ]
    away_first = [arrival[1::2], arrival[0::2]]
    order = lambda array, cells_of: jnp.stack(
        [lax.dynamic_index_in_dim(array, at, 0, keepdims=False) for at in cells_of]
    )
    rows_of = lambda array: array.reshape(group, spread).T.reshape(spread, 1, group)
    places_two = rows_of(order(token_blocks, arrival))
    starts_two = order(first_blocks, arrival)[:, 0].T.reshape(-1)
    combined = away_first[0] + away_first[1]
    places_back = pad_cols(order(token_blocks, combined).reshape(group, spread))
    starts_back = order(first_blocks, combined).reshape(-1)
    places_all = pad_cols(places)
    starts_all = first_blocks.reshape(-1)
    places_grad = rows_of(places)
    starts_grad = first_blocks[:, 0].T.reshape(-1)
    member_pad = jnp.pad(member.astype(bf16), ((0, 0), (0, LANES - experts)))
    my_expert = ((cell // per_dp) * spread + spread_at) * per_dp + cell % per_dp
    lane = jnp.arange(LANES)[None, :]
    pick = jnp.concatenate(
        [
            (lane == my_expert).astype(f32),
            (lane == experts + my_expert).astype(f32),
            jnp.zeros((6, LANES), f32),
        ],
        0,
    )
    tables = rope_tables(seq_len)
    segments = lax.dynamic_index_in_dim(segment_ids, sequence_of(row_at), 0, keepdims=True)
    seg_col = segments.reshape(seq_len, 1)
    residual = tokens_in.astype(f32)
    inv_one = inverse_rms(residual)
    normed_one = (residual * inv_one * gain_one).astype(bf16)
    raw = dot(normed_one, qkv_weight)
    query_low, key_low, value_low, heads, log_sums = attend_forward(
        raw, tables, seg_col, segments, kv_heads, block
    )
    attended = dot_nt(heads, out_weight)
    middle = lax.dynamic_slice_in_dim(residual, own_start, own_rows, 0) + sum_halves(attended)
    inv_two = inverse_rms(middle)
    normed_two = (middle * inv_two * gain_two).astype(bf16)
    half = width // 2
    pieces_two = from_cells(normed_two)
    blocks = [block for pair in pieces_two for block in pair]
    grad_sent = dispatch_grads(
        starts_grad, places_grad, grad_stack, member_pad, capacity, own_rows
    )
    grad_slots = exchange(grad_sent)
    grad_slots[0], grad_slots[1], blocks[0] = lax.optimization_barrier(
        (grad_slots[0], grad_slots[1], blocks[0])
    )

    def own_share(weight):
        split = weight.reshape((copies, spread, per_dp) + weight.shape[1:])
        return lax.dynamic_index_in_dim(split, spread_at, 1, keepdims=False).reshape(
            (cells,) + weight.shape[1:]
        )

    shares = jnp.concatenate(
        [own_share(gate_weight), own_share(up_weight), own_share(down_weight)], 1
    )
    *blocks, shares = lax.optimization_barrier((*blocks, shares))
    expert_weights = lax.all_to_all(shares, ("row", "col"), 0, 0, tiled=True)

    slots = exchange(dispatch_two(starts_two, places_two, blocks, capacity))
    results, back_a, back_b, grad_blocks = run_expert(
        slots, grad_slots, expert_weights, router_pad, pick, 2, row_count, col_count
    )

    def to_cells(back):
        return combine(starts_back, places_back, back, own_rows)

    def half_sums(own, away):
        return [own[turn].astype(f32) + away[turn].astype(f32) for turn in range(row_count)]

    def row_parts(sums):
        return [over_rows(sums[turn].astype(bf16), turn) for turn in range(1, row_count)]

    grad_got = lax.all_to_all(grad_blocks, ("row", "col"), 0, 0, tiled=True)
    kept_a, away_a = to_cells(exchange(back_a))
    away_a = lax.ppermute(away_a, "col", mirror)
    back_b = exchange(back_b)
    kept_b, away_b = to_cells(back_b)
    away_a, kept_b, away_b = lax.optimization_barrier((away_a, kept_b, away_b))
    away_b = lax.ppermute(away_b, "col", mirror)
    sums_a = half_sums(kept_a, away_a)
    parts_a = row_parts(sums_a)
    away_b, *parts_a = lax.optimization_barrier((away_b, *parts_a))
    sums_b = half_sums(kept_b, away_b)
    parts_b = row_parts(sums_b)
    own_a = sums_a[0] + sum(part.astype(f32) for part in parts_a)
    own_b = sums_b[0] + sum(part.astype(f32) for part in parts_b)
    own_a, grad_got = lax.optimization_barrier((own_a, grad_got))

    if copies > 1:
        grad_got = lax.psum_scatter(
            grad_got, "dp", scatter_dimension=0, axis_index_groups=far, tiled=True
        )
    grad_gate, grad_up, grad_down = spread_blocks(grad_got, 3)

    back_b, results = lax.optimization_barrier((back_b, results))
    results = exchange(results)
    mixed_rows = combine_add(
        own_block.reshape(1), starts_all, places_all, results, middle, row_count
    )
    own_member = lax.dynamic_slice_in_dim(member, own_block * own_rows, own_rows, 0)
    logits = jnp.where(own_member, dot(normed_two, router), masked_score)
    powers = jnp.where(own_member, jnp.exp(logits - jnp.max(logits, -1, keepdims=True)), 0.0)
    gates = powers / jnp.sum(powers, -1, keepdims=True)
    extra = own_a[:, :LANES]
    grad_gates = extra[:, :experts] + extra[:, experts : 2 * experts]
    grad_logits = (
        gates * (grad_gates - jnp.sum(gates * grad_gates, -1, keepdims=True))
    ).astype(bf16)
    grad_router = dot_tn(normed_two, grad_logits)
    grad_two = jnp.concatenate([own_a[:, LANES:], own_b], 1) + dot_nt(grad_logits, router)
    grad_norm, grad_gain_two = norm_back(grad_two, middle, inv_two, gain_two)
    own_grad = (
        lax.dynamic_slice_in_dim(grad_stack, own_block * own_rows, own_rows, 1)
        .transpose(1, 0, 2)
        .reshape(own_rows, width)
    )
    grad_middle = own_grad.astype(f32) + grad_norm

    def dp_sums(*columns):
        stacked = jnp.concatenate([column.astype(bf16) for column in columns], 1)
        stacked = jnp.pad(stacked, ((0, 0), (0, -stacked.shape[1] % LANES)))
        cols = stacked.shape[1]
        share = local_width // dp_count
        parts = stacked.reshape(row_count, dp_count, share, cols).swapaxes(0, 1)
        parts = lax.all_to_all(
            parts.reshape(dp_count, row_count * share, cols), "dp", 0, 0, tiled=True
        )
        return jnp.sum(parts.astype(f32), 0).astype(bf16).reshape(row_count, share, cols)

    def row_sums(parts):
        parts = lax.all_to_all(parts, "row", 0, 0, tiled=True)
        return jnp.sum(parts.astype(f32), 0).astype(bf16)

    grad_mid = join_halves(grad_middle.astype(bf16))
    out_sums = dp_sums(dot_tn(grad_mid, heads))
    grad_heads = dot(grad_mid, out_weight).astype(bf16)
    grad_heads, mixed_rows = lax.optimization_barrier((grad_heads, mixed_rows))
    mixed_out = lax.psum_scatter(
        mixed_rows.reshape(cells * local_rows, local_width),
        ("row", "col"),
        scatter_dimension=0,
        tiled=True,
    )
    grad_qkv = jnp.concatenate(
        attend_backward(
            query_low, key_low, value_low, log_sums, grad_heads, tables, seg_col, segments, block
        ),
        1,
    )
    grad_one = dot_nt(grad_qkv, qkv_weight)
    grad_part, grad_gain_one = norm_back(grad_one, residual, inv_one, gain_one)
    at_own = lax.dynamic_slice_in_dim(grad_part, own_start, own_rows, 0) + grad_middle
    grad_part = lax.dynamic_update_slice_in_dim(grad_part, at_own, own_start, 0)
    grad_in = from_sequences(grad_part.astype(bf16))
    qkv_sums = dp_sums(
        dot_tn(normed_one, grad_qkv), grad_router, grad_gain_two[:, None], grad_gain_one[:, None]
    )
    qkv_sums, grad_in = lax.optimization_barrier((qkv_sums, grad_in))
    summed = row_sums(jnp.concatenate([out_sums, qkv_sums], 2))
    summed, mixed_out = lax.optimization_barrier((summed, mixed_out))
    summed = lax.all_gather(summed, "dp", axis=0, tiled=True)
    also = summed[:, -LANES:]
    also = also.astype(f32) + lax.ppermute(also, "col", mirror).astype(f32)
    out_sum = summed[:, :query_cols].astype(f32)
    qkv_sum = summed[:, query_cols:-LANES].astype(f32)
    return (
        mixed_out,
        grad_in,
        also[:, experts + 1],
        qkv_sum[:, :query_cols],
        qkv_sum[:, query_cols : query_cols + key_cols],
        qkv_sum[:, query_cols + key_cols :],
        out_sum.T,
        also[:, experts],
        also[:, :experts],
        grad_gate,
        grad_up,
        grad_down,
    )


def solution(mesh):
    return jax.shard_map(
        per_device,
        mesh=mesh,
        in_specs=(
            P(("dp", "col"), "row"),
            P("row"),
            P("row", "col"),
            P("row", "col"),
            P("row", "col"),
            P("col", "row"),
            P("row"),
            P("row", None),
            P(None, "row", "col"),
            P(None, "row", "col"),
            P(None, "col", "row"),
            P("dp", None),
            P("dp", None),
            P(("dp", "col"), "row"),
        ),
        out_specs=(
            P(("dp", "col"), "row"),
            P(("dp", "col"), "row"),
            P("row"),
            P("row", "col"),
            P("row", "col"),
            P("row", "col"),
            P("col", "row"),
            P("row"),
            P("row", None),
            P("dp", "row", "col"),
            P("dp", "row", "col"),
            P("dp", "col", "row"),
        ),
        check_vma=False,
    )
```

```python
import functools

import jax
import jax.numpy as jnp
from jax import lax
from jax.experimental import pallas as pl
from jax.experimental.pallas import tpu as pltpu
from jax.sharding import PartitionSpec as P

HEAD_DIM = 64
LANES = 128

epsilon = 1e-06
rope_base = 10000.0
masked_score = -1e30

f32 = jnp.float32
bf16 = jnp.bfloat16

BIG = pltpu.CompilerParams(vmem_limit_bytes=56 * 1024 * 1024)


def dot(left, right):
    return lax.dot_general(left, right, (((1,), (0,)), ((), ())), preferred_element_type=f32)


def dot_nt(left, right):
    return lax.dot_general(left, right, (((1,), (1,)), ((), ())), preferred_element_type=f32)


def dot_tn(left, right):
    return lax.dot_general(left, right, (((0,), (0,)), ((), ())), preferred_element_type=f32)


def rope_tables(seq_len):
    midpoint = HEAD_DIM // 2
    frequency = rope_base ** (-2.0 * jnp.arange(midpoint, dtype=f32) / HEAD_DIM)
    angles = jnp.arange(seq_len, dtype=f32)[:, None] * frequency[None, :]
    cosines, sines = jnp.cos(angles), jnp.sin(angles)
    return (
        jnp.tile(cosines, (1, LANES // midpoint)),
        jnp.tile(jnp.concatenate([-sines, sines], 1), (1, LANES // HEAD_DIM)),
    )


def partner(tile):
    lane = lax.broadcasted_iota(jnp.int32, tile.shape, 1)
    half = HEAD_DIM // 2
    return jnp.where(
        (lane % HEAD_DIM) < half,
        pltpu.roll(tile, LANES - half, 1),
        pltpu.roll(tile, half, 1),
    )


def spread_pair(tile):
    tile = tile.astype(f32)
    lane = lax.broadcasted_iota(jnp.int32, tile.shape, 1)
    swapped = pltpu.roll(tile, HEAD_DIM, 1)
    low = lane < HEAD_DIM
    return (
        jnp.where(low, tile, swapped).astype(bf16),
        jnp.where(low, swapped, tile).astype(bf16),
    )


def split_heads(tile):
    lane = lax.broadcasted_iota(jnp.int32, tile.shape, 1)
    low = lane < HEAD_DIM
    zero = jnp.zeros_like(tile)
    return jnp.where(low, tile, zero), jnp.where(low, zero, tile)


def block_mask(seg_col, seg_row, start, rows, keys):
    row = lax.broadcasted_iota(jnp.int32, (rows, keys), 0) + start
    key = lax.broadcasted_iota(jnp.int32, (rows, keys), 1)
    return (key <= row) & (seg_col[start : start + rows, :] == seg_row[:, :keys])


def attend_kernel(
    query_in, key_in, value_in, cos_ref, sin_ref, col_ref, row_ref,
    query_out, key_out, value_out, heads_out, sums_out, *, block
):
    seq_len = query_in.shape[0]
    cosines, sines = cos_ref[...], sin_ref[...]
    key = key_in[...]
    key_low = (key * cosines + partner(key) * sines).astype(bf16)
    key_out[...] = key_low
    value_low = value_in[...].astype(bf16)
    value_out[...] = value_low
    keys, values = spread_pair(key_low), spread_pair(value_low)
    lane = lax.broadcasted_iota(jnp.int32, (block, LANES), 1)
    scale = 1.0 / HEAD_DIM
    for group in range(2):
        cols = slice(group * LANES, (group + 1) * LANES)
        query = query_in[:, cols]
        query_low = (query * cosines + partner(query) * sines).astype(bf16)
        query_out[:, cols] = query_low
        parts = split_heads(query_low)
        value_parts = split_heads(values[group])
        for start in range(0, seq_len, block):
            reach = start + block
            mask = block_mask(col_ref[...], row_ref[...], start, block, reach)
            total = jnp.zeros((block, LANES), f32)
            for head in range(2):
                scores = dot_nt(parts[head][start:reach], keys[group][:reach]) * scale
                scores = jnp.where(mask, scores, masked_score)
                top = jnp.max(scores, -1, keepdims=True)
                powers = jnp.exp(scores - top)
                mass = jnp.sum(powers, -1, keepdims=True)
                attention = (powers / mass).astype(bf16)
                total += dot(attention, value_parts[head][:reach])
                place = group * 2 + head
                sums = jnp.broadcast_to(top + jnp.log(mass), (block, LANES))
                if place == 0:
                    sums_out[start:reach, :] = sums
                else:
                    sums_out[start:reach, :] = jnp.where(
                        lane == place, sums, sums_out[start:reach, :]
                    )
            heads_out[start:reach, cols] = total.astype(bf16)


def attend_forward(raw, tables, seg_col, seg_row, kv_heads, block):
    seq_len = raw.shape[0]
    pairs = kv_heads // 2
    width = pairs * LANES
    spec = lambda cols, at: pl.BlockSpec((seq_len, cols), at)
    return pl.pallas_call(
        functools.partial(attend_kernel, block=block),
        grid=(pairs,),
        in_specs=[
            spec(2 * LANES, lambda i: (0, i)),
            spec(LANES, lambda i: (0, 2 * pairs + i)),
            spec(LANES, lambda i: (0, 3 * pairs + i)),
            spec(LANES, lambda i: (0, 0)),
            spec(LANES, lambda i: (0, 0)),
            pl.BlockSpec((seq_len, 1), lambda i: (0, 0)),
            pl.BlockSpec((1, seq_len), lambda i: (0, 0)),
        ],
        out_specs=[
            spec(2 * LANES, lambda i: (0, i)),
            spec(LANES, lambda i: (0, i)),
            spec(LANES, lambda i: (0, i)),
            spec(2 * LANES, lambda i: (0, i)),
            spec(LANES, lambda i: (0, i)),
        ],
        out_shape=[
            jax.ShapeDtypeStruct((seq_len, 2 * width), bf16),
            jax.ShapeDtypeStruct((seq_len, width), bf16),
            jax.ShapeDtypeStruct((seq_len, width), bf16),
            jax.ShapeDtypeStruct((seq_len, 2 * width), bf16),
            jax.ShapeDtypeStruct((seq_len, width), f32),
        ],
        compiler_params=BIG,
        name="attend_forward",
    )(raw, raw, raw, *tables, seg_col, seg_row)


def attend_back_kernel(
    query_in, key_in, value_in, sums_in, grad_in, cos_ref, sin_ref, col_ref, row_ref,
    query_out, key_out, value_out, key_sum, value_sum, *, block
):
    seq_len = query_in.shape[0]
    keys, values = spread_pair(key_in[...]), spread_pair(value_in[...])
    lane = lax.broadcasted_iota(jnp.int32, (seq_len, LANES), 1)
    low = lane < HEAD_DIM
    scale = 1.0 / HEAD_DIM
    folded = []
    for group in range(2):
        cols = slice(group * LANES, (group + 1) * LANES)
        query_parts = split_heads(query_in[:, cols])
        grad_parts = split_heads(grad_in[:, cols])
        key_parts = split_heads(keys[group])
        key_sum[...] = jnp.zeros_like(key_sum)
        value_sum[...] = jnp.zeros_like(value_sum)
        for start in range(0, seq_len, block):
            reach = start + block
            rows = slice(start, reach)
            mask = block_mask(col_ref[...], row_ref[...], start, block, reach)
            total = jnp.zeros((block, LANES), f32)
            for head in range(2):
                place = group * 2 + head
                query, grad = query_parts[head][rows], grad_parts[head][rows]
                scores = dot_nt(query, keys[group][:reach]) * scale
                powers = jnp.exp(scores - sums_in[rows, place : place + 1])
                attention = jnp.where(mask, powers, 0.0)
                value_sum[:reach, :] += dot_tn(attention.astype(bf16), grad)
                grad_probs = dot_nt(grad, values[group][:reach])
                inner = jnp.sum(grad_probs * attention, -1, keepdims=True)
                grad_scores = (attention * (grad_probs - inner) * scale).astype(bf16)
                key_sum[:reach, :] += dot_tn(grad_scores, query)
                total += dot(grad_scores, key_parts[head][:reach])
            cosines, sines = cos_ref[rows, :], sin_ref[rows, :]
            query_out[rows, cols] = (total * cosines - partner(total) * sines).astype(bf16)
        grad_key, grad_value = key_sum[...], value_sum[...]
        folded.append(
            (
                grad_key + pltpu.roll(grad_key, HEAD_DIM, 1),
                grad_value + pltpu.roll(grad_value, HEAD_DIM, 1),
            )
        )
    grad_key = jnp.where(low, folded[0][0], folded[1][0])
    grad_value = jnp.where(low, folded[0][1], folded[1][1])
    key_out[...] = (grad_key * cos_ref[...] - partner(grad_key) * sin_ref[...]).astype(bf16)
    value_out[...] = grad_value.astype(bf16)


def in_vmem(count):
    return [pl.BlockSpec(memory_space=pltpu.VMEM) for _ in range(count)]


def weight_products_kernel(mid_ref, heads_ref, small_ref, left_ref, *refs):
    *right_refs, out_ref = refs
    start = heads_ref.shape[1]
    out_ref[:, :start] = dot_tn(mid_ref[...], heads_ref[...]).astype(bf16)
    out_ref[:, start : start + LANES] = small_ref[...]
    start += LANES
    for right in right_refs:
        stop = start + right.shape[1]
        out_ref[:, start:stop] = dot_tn(left_ref[...], right[...]).astype(bf16)
        start = stop


def weight_products(mid, heads, small, left, rights):
    cols = heads.shape[1] + LANES + sum(right.shape[1] for right in rights)
    return pl.pallas_call(
        weight_products_kernel,
        in_specs=in_vmem(4 + len(rights)),
        out_specs=in_vmem(1)[0],
        out_shape=jax.ShapeDtypeStruct((left.shape[1], cols), bf16),
        compiler_params=BIG,
        name="weight_products",
    )(mid, heads, small, left, *rights)


def attend_backward(query, key, value, sums, grad, tables, seg_col, seg_row, block):
    seq_len = query.shape[0]
    width = key.shape[1]
    pairs = width // LANES
    spec = lambda cols, at: pl.BlockSpec((seq_len, cols), at)
    here = lambda i: (0, i)
    first = lambda i: (0, 0)
    return pl.pallas_call(
        functools.partial(attend_back_kernel, block=block),
        grid=(pairs,),
        in_specs=[
            spec(2 * LANES, here),
            spec(LANES, here),
            spec(LANES, here),
            spec(LANES, here),
            spec(2 * LANES, here),
            spec(LANES, first),
            spec(LANES, first),
            pl.BlockSpec((seq_len, 1), first),
            pl.BlockSpec((1, seq_len), first),
        ],
        out_specs=[spec(2 * LANES, here), spec(LANES, here), spec(LANES, here)],
        out_shape=[
            jax.ShapeDtypeStruct((seq_len, 2 * width), bf16),
            jax.ShapeDtypeStruct((seq_len, width), bf16),
            jax.ShapeDtypeStruct((seq_len, width), bf16),
        ],
        scratch_shapes=[pltpu.VMEM((seq_len, LANES), f32), pltpu.VMEM((seq_len, LANES), f32)],
        compiler_params=BIG,
        name="attend_backward",
    )(query, key, value, sums, grad, *tables, seg_col, seg_row)


def place_rows_of(place_ref, starts_ref, which, tokens, window, capacity):
    start = starts_ref[which]
    start = pl.multiple_of(jnp.minimum(start - start % 16, capacity - window), 16)
    slots = lax.broadcasted_iota(jnp.int32, (window, tokens), 0) + start
    return start, jnp.where(slots == place_ref, 1.0, 0.0).astype(bf16)


def store_at(step, refs, value):
    for index, ref in enumerate(refs):

        @pl.when(step == index)
        def _():
            ref[...] = value


def dispatch_two_kernel(starts_ref, place_ref, *refs, count):
    blocks, out_refs, total = refs[: -1 - count], refs[-1 - count : -1], refs[-1]
    tokens = blocks[0].shape[0]
    capacity = total.shape[0]
    window = tokens + 16
    expert = pl.program_id(0)
    total[...] = jnp.zeros_like(total)
    for index, block in enumerate(blocks):
        start, chosen = place_rows_of(
            place_ref[0, :, index * tokens : (index + 1) * tokens],
            starts_ref,
            expert * len(blocks) + index,
            tokens,
            window,
            capacity,
        )
        total[pl.ds(start, window), :] += dot(chosen, block[...])
    store_at(expert, out_refs, total[...].astype(bf16))


def dispatch_grads_kernel(starts_ref, place_ref, stack_ref, member_ref, *refs, block):
    *out_refs, total = refs
    parts, tokens, width = stack_ref.shape
    capacity = total.shape[0]
    window = block + 16
    expert = pl.program_id(0)
    total[...] = jnp.zeros_like(total)
    steps = tokens // block
    for step in range(steps):
        rows = slice(step * block, (step + 1) * block)
        start, chosen = place_rows_of(
            place_ref[0, :, rows], starts_ref, expert * steps + step, block, window, capacity
        )
        values = jnp.concatenate(
            [stack_ref[part, rows, :] for part in range(parts)] + [member_ref[rows, :]], 1
        )
        total[pl.ds(start, window), :] += dot(chosen, values)
    store_at(expert, out_refs, total[...].astype(bf16))


def dispatch(kernel, name, starts, places, arrays, capacity, width):
    count, _, tokens = places.shape
    whole = lambda array: pl.BlockSpec(array.shape, lambda i: (0,) * array.ndim)
    return pl.pallas_call(
        kernel,
        grid=(count,),
        in_specs=[
            pl.BlockSpec(memory_space=pltpu.SMEM),
            pl.BlockSpec((1, 1, tokens), lambda i: (i, 0, 0)),
        ]
        + [whole(array) for array in arrays],
        out_specs=[pl.BlockSpec((capacity, width), lambda i: (0, 0))] * count,
        out_shape=[jax.ShapeDtypeStruct((capacity, width), bf16)] * count,
        scratch_shapes=[pltpu.VMEM((capacity, width), f32)],
        compiler_params=BIG,
        name=name,
    )(starts, places, *arrays)


def dispatch_two(starts, places, blocks, capacity):
    count = places.shape[0]
    kernel = functools.partial(dispatch_two_kernel, count=count)
    width = blocks[0].shape[1]
    return dispatch(kernel, "dispatch_tokens", starts, places, blocks, capacity, width)


def dispatch_grads(starts, places, stack, members, capacity, block):
    kernel = functools.partial(dispatch_grads_kernel, block=block)
    width = stack.shape[0] * stack.shape[2] + LANES
    return dispatch(
        kernel, "dispatch_grads", starts, places, [stack, members], capacity, width
    )


def gather_back(starts_ref, place_ref, value_refs, which, capacity):
    tokens = place_ref.shape[0]
    window = 2 * tokens
    count = len(value_refs)
    total = None
    for expert, values_ref in enumerate(value_refs):
        start = starts_ref[which * count + expert]
        start = pl.multiple_of(jnp.minimum(start - start % 16, capacity - window), 16)
        slots = lax.broadcasted_iota(jnp.int32, (tokens, window), 1) + start
        chosen = jnp.where(slots == place_ref[:, expert : expert + 1], 1.0, 0.0).astype(bf16)
        term = dot(chosen, values_ref[pl.ds(start, window), :])
        total = term if total is None else total + term
    return total


def combine_kernel(starts_ref, place_ref, *refs, capacity):
    *value_refs, own_ref, away_ref = refs
    step = pl.program_id(0)
    half = pl.num_programs(0) // 2
    pieces = place_ref.shape[0] // LANES
    for piece in range(pieces):
        rows = slice(piece * LANES, (piece + 1) * LANES)
        total = gather_back(
            starts_ref, place_ref[rows, :], value_refs, step * pieces + piece, capacity
        ).astype(bf16)

        @pl.when(step < half)
        def _():
            away_ref[0, rows, :] = total

        @pl.when(step >= half)
        def _():
            own_ref[0, rows, :] = total


def combine(starts, places, values, block):
    tokens = places.shape[0]
    capacity, width = values[0].shape
    half = tokens // block // 2
    out = jax.ShapeDtypeStruct((half, block, width), bf16)
    return pl.pallas_call(
        functools.partial(combine_kernel, capacity=capacity),
        grid=(2 * half,),
        in_specs=[
            pl.BlockSpec(memory_space=pltpu.SMEM),
            pl.BlockSpec((block, LANES), lambda i: (i, 0)),
        ]
        + [pl.BlockSpec((capacity, width), lambda i: (0, 0)) for _ in values],
        out_specs=[
            pl.BlockSpec((1, block, width), lambda i: (jnp.maximum(i - half, 0), 0, 0)),
            pl.BlockSpec((1, block, width), lambda i: (jnp.minimum(i, half - 1), 0, 0)),
        ],
        out_shape=[out, out],
        compiler_params=BIG,
        name="combine_rows",
    )(starts, places, *values)


def combine_add_kernel(own_ref, starts_ref, place_ref, add_ref, *refs, capacity):
    *value_refs, out_ref = refs
    step = pl.program_id(0)
    factor = jnp.where(step == own_ref[0], 1.0, 0.0)
    parts, block, width = out_ref.shape
    pieces = block // LANES
    for piece in range(pieces):
        rows = slice(piece * LANES, (piece + 1) * LANES)
        total = gather_back(
            starts_ref, place_ref[rows, :], value_refs, step * pieces + piece, capacity
        )
        total += add_ref[rows, :] * factor
        for part in range(parts):
            out_ref[part, rows, :] = total[:, part * width : (part + 1) * width].astype(bf16)


def combine_add(own, starts, places, values, addition, parts):
    tokens = places.shape[0]
    capacity, width = values[0].shape
    block = addition.shape[0]
    return pl.pallas_call(
        functools.partial(combine_add_kernel, capacity=capacity),
        grid=(tokens // block,),
        in_specs=[
            pl.BlockSpec(memory_space=pltpu.SMEM),
            pl.BlockSpec(memory_space=pltpu.SMEM),
            pl.BlockSpec((block, LANES), lambda i: (i, 0)),
            pl.BlockSpec((block, width), lambda i: (0, 0)),
        ]
        + [pl.BlockSpec((capacity, width), lambda i: (0, 0)) for _ in values],
        out_specs=pl.BlockSpec((parts, block, width // parts), lambda i: (0, i, 0)),
        out_shape=jax.ShapeDtypeStruct((parts, tokens, width // parts), bf16),
        compiler_params=BIG,
        name="combine_rows_add",
    )(own, starts, places, addition, *values)


def weight_blocks(row_count, col_count, part, hidden_cols):
    for row in range(row_count):
        for col in range(col_count):
            rows = slice(row * part, (row + 1) * part)
            cols = slice(col * part, (col + 1) * part)
            above = slice(hidden_cols + col * part, hidden_cols + (col + 1) * part)
            yield row * col_count + col, rows, cols, above


def expert_kernel(
    weight_ref, router_ref, pick_ref, *refs, groups, row_count, col_count
):
    slot_refs, grad_refs = refs[:groups], refs[groups : 2 * groups]
    out_refs, back_a_refs, back_b_refs = (
        refs[at * groups : (at + 1) * groups] for at in (2, 3, 4)
    )
    save_refs = refs[5 * groups : 6 * groups]
    up_ref, down_ref, slot_ref, grad_ref = refs[6 * groups :]
    step = pl.program_id(0) * pl.num_programs(1) + pl.program_id(1)
    width = slot_ref.shape[1]
    split = back_b_refs[0].shape[1]
    for group in range(groups):

        @pl.when(pl.program_id(0) == group)
        def _():
            slot_ref[...] = slot_refs[group][...]
            grad_ref[...] = grad_refs[group][...]

    hidden_cols = down_ref.shape[0]
    part = weight_ref.shape[2]

    @pl.when(step == 0)
    def _():
        for cell, rows, cols, above in weight_blocks(row_count, col_count, part, hidden_cols):
            up_ref[rows, cols] = weight_ref[cell, :part, :]
            up_ref[rows, above] = weight_ref[cell, part : 2 * part, :]
            down_ref[cols, rows] = weight_ref[cell, 2 * part :, :]

    slots = slot_ref[...]
    grads = grad_ref[:, :width].astype(f32)
    member = grad_ref[:, width:].astype(f32) > 0.5
    logits = jnp.where(member, dot(slots, router_ref[...]), masked_score)
    top = jnp.max(logits, -1, keepdims=True)
    powers = jnp.where(member, jnp.exp(logits - top), 0.0)
    mass = jnp.sum(powers, -1, keepdims=True)
    pick = pick_ref[...]
    gate = jnp.sum(powers * pick[0:1, :], -1, keepdims=True) / jnp.maximum(mass, 1e-30)
    both = dot(slots, up_ref[...])
    gate_part, up_part = both[:, :hidden_cols], both[:, hidden_cols:]
    sigmoid = 1.0 / (1.0 + jnp.exp(-gate_part))
    silu = gate_part * sigmoid
    hidden = (silu * up_part).astype(bf16)
    result = dot(hidden, down_ref[...])
    scaled = (result * gate).astype(bf16)
    dots = jnp.sum(result * grads, -1, keepdims=True)
    dots_high = dots.astype(bf16).astype(f32)
    dots_low = dots - dots_high
    split_dots = (dots_high * pick[0:1, :] + dots_low * pick[1:2, :]).astype(bf16)
    grad_expert = (grads * gate).astype(bf16)
    grad_hidden = dot_nt(grad_expert, down_ref[...])
    grad_pair = jnp.concatenate(
        [
            grad_hidden * up_part * sigmoid * (1.0 + gate_part * (1.0 - sigmoid)),
            grad_hidden * silu,
        ],
        1,
    ).astype(bf16)
    back = dot_nt(grad_pair, up_ref[...]).astype(bf16)
    for group in range(groups):

        @pl.when(pl.program_id(0) == group)
        def _():
            out_refs[group][...] = scaled
            back_a_refs[group][:, :LANES] = split_dots
            back_a_refs[group][:, LANES:] = back[:, : width - split]
            back_b_refs[group][...] = back[:, width - split :]
            save_refs[group][:, :hidden_cols] = hidden
            save_refs[group][:, hidden_cols : hidden_cols + width] = grad_expert
            save_refs[group][:, hidden_cols + width :] = grad_pair


def expert_grads_kernel(*refs, groups, row_count, col_count):
    slot_refs, save_refs, out_ref = refs[:groups], refs[groups : 2 * groups], refs[2 * groups]
    part = out_ref.shape[2]
    width = slot_refs[0].shape[1]
    hidden_cols = col_count * part
    first_pair = hidden_cols + width

    def product(lefts, left_cols, rights, right_cols):
        terms = [
            dot_tn(left[:, left_cols], right[:, right_cols]) for left, right in zip(lefts, rights)
        ]
        return sum(terms).astype(bf16)

    for cell, rows, cols, above in weight_blocks(row_count, col_count, part, hidden_cols):
        for place, pair in enumerate((cols, above)):
            pair = slice(first_pair + pair.start, first_pair + pair.stop)
            out_ref[cell, place * part : (place + 1) * part, :] = product(
                slot_refs, rows, save_refs, pair
            )
        out = slice(hidden_cols + rows.start, hidden_cols + rows.stop)
        out_ref[cell, 2 * part :, :] = product(save_refs, cols, save_refs, out)


def expert_grads(slots, saved, shape, row_count, col_count):
    groups = len(slots)
    return pl.pallas_call(
        functools.partial(
            expert_grads_kernel, groups=groups, row_count=row_count, col_count=col_count
        ),
        in_specs=in_vmem(2 * groups),
        out_specs=in_vmem(1)[0],
        out_shape=jax.ShapeDtypeStruct(shape, bf16),
        compiler_params=BIG,
        name="expert_grads",
    )(*slots, *saved)


def run_expert(slots, grads, weights, router, pick, steps, row_count, col_count):
    groups = len(slots)
    capacity, width = slots[0].shape
    rest = grads[0].shape[1]
    half = width // 2
    block = capacity // steps
    hidden_cols = weights.shape[2] * col_count
    kept = 3 * hidden_cols + width
    whole = lambda shape: pl.BlockSpec(shape, lambda i, j: (0,) * len(shape))

    def some(cols):
        def spec(group):
            return pl.BlockSpec(
                (block, cols),
                lambda i, j: (
                    jnp.where(i < group, 0, jnp.where(i > group, steps - 1, j)),
                    0,
                ),
            )

        return [spec(group) for group in range(groups)]

    shapes = lambda cols: [jax.ShapeDtypeStruct((capacity, cols), bf16)] * groups
    outs = pl.pallas_call(
        functools.partial(
            expert_kernel, groups=groups, row_count=row_count, col_count=col_count
        ),
        grid=(groups, steps),
        in_specs=[whole(weights.shape), whole(router.shape), whole(pick.shape)]
        + some(width)
        + some(rest),
        out_specs=some(width) + some(half + LANES) + some(half) + some(kept),
        out_shape=shapes(width)
        + shapes(half + LANES)
        + shapes(half)
        + shapes(kept),
        scratch_shapes=[
            pltpu.VMEM((width, 2 * hidden_cols), bf16),
            pltpu.VMEM((hidden_cols, width), bf16),
            pltpu.VMEM((block, width), bf16),
            pltpu.VMEM((block, rest), bf16),
        ],
        compiler_params=BIG,
        name="expert_pass",
    )(weights, router, pick, *slots, *grads)
    return (
        outs[:groups],
        outs[groups : 2 * groups],
        outs[2 * groups : 3 * groups],
        outs[3 * groups :],
    )


def spread_kernel(block_ref, *out_refs):
    part = out_refs[0].shape[1]
    for index, out_ref in enumerate(out_refs):
        out_ref[0] = block_ref[0, index * part : (index + 1) * part, :].astype(f32)


def spread_blocks(blocks, count):
    cells, rows, cols = blocks.shape
    part = rows // count
    return pl.pallas_call(
        spread_kernel,
        grid=(cells,),
        in_specs=[pl.BlockSpec((1, rows, cols), lambda i: (i, 0, 0))],
        out_specs=[pl.BlockSpec((1, part, cols), lambda i: (i, 0, 0))] * count,
        out_shape=[jax.ShapeDtypeStruct((cells, part, cols), f32)] * count,
        compiler_params=BIG,
        name="spread_blocks",
    )(blocks)


def norm_back(grad, values, inv_rms, gain):
    scaled = grad * gain
    inner = jnp.mean(scaled * values, -1, keepdims=True)
    grad_gain = jnp.sum(grad * values * inv_rms, 0)
    return (inv_rms * scaled - values * inv_rms * inv_rms * inv_rms * inner, grad_gain)


def inverse_rms(values):
    return lax.rsqrt(jnp.mean(values * values, -1, keepdims=True) + epsilon)


def running_count(member):
    tokens, cols = member.shape
    chunk = LANES
    parts = member.reshape(tokens // chunk, chunk, cols)
    lower = jnp.tril(jnp.ones((chunk, chunk), f32))
    inside = jnp.einsum("ij,bjc->bic", lower, parts, preferred_element_type=f32)
    sums = jnp.sum(parts, 1)
    blocks = tokens // chunk
    before = jnp.sum(
        jnp.where(
            jnp.arange(blocks)[:, None, None] > jnp.arange(blocks)[None, :, None],
            sums[None, :, :],
            0.0,
        ),
        1,
    )
    return (inside + before[:, None, :]).reshape(tokens, cols).astype(jnp.int32)


def per_device(
    hidden_in,
    norm1_gain,
    query_weight,
    key_weight,
    value_weight,
    output_weight,
    norm2_gain,
    router_weight,
    gate_weight,
    up_weight,
    down_weight,
    segment_ids,
    expert_ids,
    grad_out,
):
    dp_count = lax.axis_size("dp")
    row_count = lax.axis_size("row")
    col_count = lax.axis_size("col")
    dp_at, row_at, col_at = (lax.axis_index(name) for name in ("dp", "row", "col"))
    cell = row_at * col_count + col_at
    cells = row_count * col_count
    local_rows, local_width = hidden_in.shape
    group, chosen = expert_ids.shape
    width = local_width * row_count
    experts = gate_weight.shape[0]
    hidden_part = gate_weight.shape[2]
    hidden_cols = hidden_part * col_count
    capacity = group * chosen * 5 // (4 * experts)
    sequences, seq_len = segment_ids.shape
    own_rows = seq_len // col_count
    query_cols, key_cols = query_weight.shape[1], key_weight.shape[1]
    kv_heads = key_cols // HEAD_DIM
    block = seq_len // 2
    spread = experts // cells
    copies = dp_count // spread
    per_dp = experts // dp_count
    assert sequences == row_count and spread * cells == experts and copies * spread == dp_count
    spread_at = dp_at % spread
    if copies == 1:
        far = None
    else:
        far = [[i * spread + j for i in range(copies)] for j in range(spread)]

    def exchange(arrays):
        return [over_dp(array, turn) for turn, array in enumerate(arrays)]

    def by_cell(array):
        lead = array.shape[:-1]
        split = array.reshape(lead + (copies, spread, per_dp))
        return jnp.swapaxes(split, -3, -2).reshape(lead + (spread, cells))

    per_col = sequences // col_count
    part_at = (row_at // col_count) * col_count + col_at
    sequence_of = lambda row: (row % col_count) * per_col + row // col_count
    block_of = lambda row, col: sequence_of(row) * col_count + col
    own_block = block_of(row_at, col_at)

    def rounds():
        for turn in range(row_count):
            there, back = [], []
            for row in range(row_count):
                for col in range(col_count):
                    part = (row - turn) % row_count
                    other = ((part // col_count) * col_count + col) * col_count + part % col_count
                    there.append((row * col_count + col, other))
                    back.append((other, row * col_count + col))
            yield turn, there, back

    def to_sequences(array):
        parts = array.reshape(per_col, seq_len, local_width)
        got = []
        for turn, there, _ in rounds():
            part = (row_at - turn) % row_count
            own = lax.dynamic_index_in_dim(parts, part // col_count, 0, keepdims=False)
            got.append(lax.ppermute(own, ("row", "col"), there))
        got = jnp.stack(got)
        return jnp.concatenate(
            [
                lax.dynamic_index_in_dim(got, (row - part_at) % row_count, 0, keepdims=False)
                for row in range(row_count)
            ],
            1,
        )

    def from_sequences(array):
        parts = array.reshape(seq_len, row_count, local_width).transpose(1, 0, 2)
        got = []
        for turn, _, back in rounds():
            own = lax.dynamic_index_in_dim(
                parts, (turn + part_at) % row_count, 0, keepdims=False
            )
            got.append(lax.ppermute(own, ("row", "col"), back).astype(f32))
        total = []
        for index in range(per_col):
            total.append(
                sum(
                    jnp.where(((row_at - turn) % row_count) // col_count == index, got[turn], 0.0)
                    for turn in range(row_count)
                )
            )
        return jnp.concatenate(total, 0)

    own_start = col_at * own_rows
    mirror = [(col, col_count - 1 - col) for col in range(col_count)]

    def sum_halves(array):
        parts = array.reshape(col_count, own_rows, array.shape[1])
        away = lax.dynamic_index_in_dim(parts, 1 - col_at, 0, keepdims=False).astype(bf16)
        own = lax.dynamic_index_in_dim(parts, col_at, 0, keepdims=False)
        return own + lax.ppermute(away, "col", mirror).astype(f32)

    def join_halves(array):
        other = lax.ppermute(array, "col", mirror)
        first = col_at == 0
        return jnp.concatenate(
            [jnp.where(first, array, other), jnp.where(first, other, array)], 0
        )

    def in_terms(array):
        terms = []
        for _ in range(3):
            terms.append(array.astype(bf16))
            array = array - terms[-1].astype(f32)
        return terms

    tokens_in = to_sequences(hidden_in)
    extras = jnp.concatenate(
        [router_weight, jnp.stack(in_terms(norm1_gain) + in_terms(norm2_gain), 1)], 1
    )
    def over_rows(array, turn):
        pairs = [(row, row ^ turn) for row in range(row_count)]
        return lax.ppermute(array, "row", pairs) if turn else array

    def over_dp(array, turn):
        pairs = [(at, at ^ turn) for at in range(dp_count)]
        return lax.ppermute(array, "dp", pairs) if turn else array

    def over_cells(array, turn):
        pairs = [(at, at ^ turn) for at in range(cells)]
        return lax.ppermute(array, ("row", "col"), pairs) if turn else array

    pick_from = lambda array, at: lax.dynamic_index_in_dim(array, at, 0, keepdims=False)

    def all_rows(array):
        share = local_width // spread
        own = lax.dynamic_slice_in_dim(array, spread_at * share, share, 0)
        rows = jnp.stack([over_rows(own, turn) for turn in range(row_count)])
        rows = jnp.stack([pick_from(rows, row_at ^ row) for row in range(row_count)])
        shares = jnp.stack([over_dp(rows, turn) for turn in range(spread)])
        ordered = jnp.stack([pick_from(shares, spread_at ^ at) for at in range(spread)], 1)
        return ordered.reshape(width, array.shape[1])

    qkv_cols = query_cols + 2 * key_cols
    first_weights = all_rows(
        jnp.concatenate(
            [
                query_weight,
                key_weight,
                value_weight,
                jnp.pad(extras, ((0, 0), (0, LANES - extras.shape[1]))),
            ],
            1,
        )
    )
    first_weights, out_late = lax.optimization_barrier((first_weights, output_weight))
    out_weight = all_rows(out_late.T)
    grad_stack = lax.all_gather(grad_out, ("row", "col"), axis=0, tiled=True).reshape(
        row_count, group, local_width
    )

    qkv_weight = first_weights[:, :qkv_cols]
    extras = first_weights[:, qkv_cols:]
    router_pad = jnp.where(jnp.arange(LANES)[None, :] < experts, extras, jnp.zeros((), bf16))
    router = extras[:, :experts]
    terms = extras[:, experts : experts + 6].astype(f32)
    gain_one = (terms[:, 0] + terms[:, 1] + terms[:, 2])[None, :]
    gain_two = (terms[:, 3] + terms[:, 4] + terms[:, 5])[None, :]
    def from_rows(array):
        return [over_rows(array, turn) for turn in range(row_count)]

    def from_columns(rows):
        return [block for row in rows for block in (row, lax.ppermute(row, "col", mirror))]

    member = jnp.any(
        expert_ids[:, :, None] == jnp.arange(experts, dtype=jnp.int32)[None, None, :], 1
    )
    mine = lax.dynamic_index_in_dim(
        by_cell(member.astype(f32)), cell, 2, keepdims=False
    )
    mine = jnp.concatenate(
        [lax.dynamic_slice_in_dim(mine, spread_at ^ turn, 1, 1) for turn in range(spread)], 1
    )
    places = jnp.where(mine > 0.5, running_count(mine) - 1, -1)
    first = running_count(mine) - mine.astype(jnp.int32)
    token_blocks = places.reshape(cells, own_rows, spread)
    first_blocks = first.reshape(cells, own_rows, spread)[:, ::LANES]
    pad_cols = lambda array: jnp.pad(
        array, ((0, 0), (0, LANES - spread)), constant_values=-1
    )
    arrival = [
        block_of(row_at ^ turn, col_at ^ side)
        for turn in range(row_count)
        for side in range(2)
    ]
    away_first = [arrival[1::2], arrival[0::2]]
    order = lambda array, cells_of: jnp.stack(
        [lax.dynamic_index_in_dim(array, at, 0, keepdims=False) for at in cells_of]
    )
    rows_of = lambda array: array.reshape(group, spread).T.reshape(spread, 1, group)
    places_two = rows_of(order(token_blocks, arrival))
    starts_two = order(first_blocks, arrival)[:, 0].T.reshape(-1)
    combined = away_first[0] + away_first[1]
    places_back = pad_cols(order(token_blocks, combined).reshape(group, spread))
    starts_back = order(first_blocks, combined).reshape(-1)
    places_all = pad_cols(places)
    starts_all = first_blocks.reshape(-1)
    places_grad = rows_of(places)
    starts_grad = first_blocks[:, 0].T.reshape(-1)
    member_pad = jnp.pad(member.astype(bf16), ((0, 0), (0, LANES - experts)))
    my_expert = ((cell // per_dp) * spread + spread_at) * per_dp + cell % per_dp
    lane = jnp.arange(LANES)[None, :]
    pick = jnp.concatenate(
        [
            (lane == my_expert).astype(f32),
            (lane == experts + my_expert).astype(f32),
            jnp.zeros((6, LANES), f32),
        ],
        0,
    )
    tables = rope_tables(seq_len)
    segments = lax.dynamic_index_in_dim(segment_ids, sequence_of(row_at), 0, keepdims=True)
    seg_col = segments.reshape(seq_len, 1)
    residual = tokens_in.astype(f32)
    inv_one = inverse_rms(residual)
    normed_one = (residual * inv_one * gain_one).astype(bf16)
    raw = dot(normed_one, qkv_weight)
    query_low, key_low, value_low, heads, log_sums = attend_forward(
        raw, tables, seg_col, segments, kv_heads, block
    )
    attended = dot_nt(heads, out_weight)
    middle = lax.dynamic_slice_in_dim(residual, own_start, own_rows, 0) + sum_halves(attended)
    inv_two = inverse_rms(middle)
    normed_two = (middle * inv_two * gain_two).astype(bf16)
    half = width // 2
    early = spread - 1
    grad_slots = exchange(
        dispatch_grads(starts_grad, places_grad, grad_stack, member_pad, capacity, own_rows)
    )
    normed_sent, *grad_slots[:2] = lax.optimization_barrier((normed_two, *grad_slots[:2]))
    blocks = from_columns(from_rows(normed_sent))
    blocks[0], *grad_slots = lax.optimization_barrier((blocks[0], *grad_slots))

    def own_share(weight):
        split = weight.reshape((copies, spread, per_dp) + weight.shape[1:])
        return lax.dynamic_index_in_dim(split, spread_at, 1, keepdims=False).reshape(
            (cells,) + weight.shape[1:]
        )

    shares = jnp.concatenate(
        [own_share(gate_weight), own_share(up_weight), own_share(down_weight)], 1
    )
    *blocks, shares = lax.optimization_barrier((*blocks, shares))
    expert_weights = lax.all_to_all(shares, ("row", "col"), 0, 0, tiled=True)

    slots = exchange(dispatch_two(starts_two, places_two, blocks, capacity))
    results, back_a, back_b, saved = run_expert(
        slots, grad_slots, expert_weights, router_pad, pick, 2, row_count, col_count
    )

    def to_cells(back):
        return combine(starts_back, places_back, back, own_rows)

    def half_sums(own, away):
        return [own[turn].astype(f32) + away[turn].astype(f32) for turn in range(row_count)]

    def row_parts(sums):
        return [over_rows(sums[turn].astype(bf16), turn) for turn in range(1, row_count)]

    back_a, saved = exchange(back_a), list(saved)
    back_b = exchange(back_b)
    *back_a[:2], saved[0] = lax.optimization_barrier((*back_a[:2], saved[0]))
    back_a[0], *back_b[:early] = lax.optimization_barrier((back_a[0], *back_b[:early]))
    kept_a, away_a = to_cells(back_a)
    grad_blocks = expert_grads(slots, saved, shares.shape, row_count, col_count)
    grad_got = lax.all_to_all(grad_blocks, ("row", "col"), 0, 0, tiled=True)
    away_a = lax.ppermute(away_a, "col", mirror)
    kept_b, away_b = to_cells(back_b)
    away_a, kept_b, away_b = lax.optimization_barrier((away_a, kept_b, away_b))
    away_b = lax.ppermute(away_b, "col", mirror)
    sums_a = half_sums(kept_a, away_a)
    parts_a = row_parts(sums_a)
    back_b[0], *results = lax.optimization_barrier((back_b[0], *results))
    results = exchange(results)
    away_b, parts_a, results[:early] = lax.optimization_barrier(
        (away_b, parts_a, results[:early])
    )
    sums_b = half_sums(kept_b, away_b)
    parts_b = row_parts(sums_b)
    mixed_rows = combine_add(
        own_block.reshape(1), starts_all, places_all, results, middle, row_count
    )
    parts_b, mixed_rows = lax.optimization_barrier((parts_b, mixed_rows))
    own_a = sums_a[0] + sum(part.astype(f32) for part in parts_a)
    own_b = sums_b[0] + sum(part.astype(f32) for part in parts_b)

    if copies > 1:
        grad_got = lax.psum_scatter(
            grad_got, "dp", scatter_dimension=0, axis_index_groups=far, tiled=True
        )

    own_member = lax.dynamic_slice_in_dim(member, own_block * own_rows, own_rows, 0)
    logits = jnp.where(own_member, dot(normed_two, router), masked_score)
    powers = jnp.where(own_member, jnp.exp(logits - jnp.max(logits, -1, keepdims=True)), 0.0)
    gates = powers / jnp.sum(powers, -1, keepdims=True)
    extra = own_a[:, :LANES]
    grad_gates = extra[:, :experts] + extra[:, experts : 2 * experts]
    grad_logits = (
        gates * (grad_gates - jnp.sum(gates * grad_gates, -1, keepdims=True))
    ).astype(bf16)
    grad_router = dot_tn(normed_two, grad_logits)
    grad_two = jnp.concatenate([own_a[:, LANES:], own_b], 1) + dot_nt(grad_logits, router)
    grad_norm, grad_gain_two = norm_back(grad_two, middle, inv_two, gain_two)
    own_grad = (
        lax.dynamic_slice_in_dim(grad_stack, own_block * own_rows, own_rows, 1)
        .transpose(1, 0, 2)
        .reshape(own_rows, width)
    )
    grad_middle = own_grad.astype(f32) + grad_norm

    share_rows = local_width // dp_count
    by_share = lambda array: array.reshape(
        array.shape[0], row_count, dp_count, share_rows
    ).swapaxes(1, 2).reshape(array.shape)

    def dp_sums(stacked):
        parts = stacked.reshape(dp_count, row_count * share_rows, stacked.shape[1])
        parts = lax.all_to_all(parts, "dp", 0, 0, tiled=True)
        summed = jnp.sum(parts.astype(f32), 0)
        return summed.reshape(row_count, share_rows, stacked.shape[1])

    def row_sums(parts):
        parts = lax.all_to_all(parts, "row", 0, 0, tiled=True)
        return jnp.sum(parts.astype(f32), 0)

    def in_two(array):
        high = array.astype(bf16)
        low = (array - high.astype(f32)).astype(bf16)
        pad = ((0, 0),) * (array.ndim - 1) + ((0, LANES - 2 * array.shape[-1]),)
        return jnp.pad(jnp.concatenate([high, low], -1), pad)

    smalls = experts + 1
    of_two = lambda array: array[..., :smalls] + array[..., smalls : 2 * smalls]

    grad_mid = join_halves(grad_middle.astype(bf16))
    grad_mid, grad_got = lax.optimization_barrier((grad_mid, grad_got))
    grad_gate, grad_up, grad_down = spread_blocks(grad_got, 3)
    small = jnp.concatenate([grad_router, grad_gain_two[:, None]], 1)
    grad_heads = dot(grad_mid, out_weight).astype(bf16)
    grad_heads, mixed_rows = lax.optimization_barrier((grad_heads, mixed_rows))
    mixed_out = lax.psum_scatter(
        mixed_rows.reshape(cells * local_rows, local_width),
        ("row", "col"),
        scatter_dimension=0,
        tiled=True,
    )
    grad_qkv = attend_backward(
        query_low, key_low, value_low, log_sums, grad_heads, tables, seg_col, segments, block
    )
    small = in_two(by_share(small.T).T)
    sums = dp_sums(
        weight_products(by_share(grad_mid), heads, small, by_share(normed_one), grad_qkv)
    )
    grad_qkv = jnp.concatenate(grad_qkv, 1)
    grad_one = dot_nt(grad_qkv, qkv_weight)
    grad_part, _ = norm_back(grad_one, residual, inv_one, gain_one)
    at_own = lax.dynamic_slice_in_dim(grad_part, own_start, own_rows, 0) + grad_middle
    grad_part = lax.dynamic_update_slice_in_dim(grad_part, at_own, own_start, 0)
    grad_in = from_sequences(grad_part.astype(bf16))
    main = query_cols + LANES

    def rounded(sums):
        return jnp.concatenate(
            [
                sums[..., :query_cols].astype(bf16),
                in_two(of_two(sums[..., query_cols:main])),
                sums[..., main:].astype(bf16),
            ],
            -1,
        )

    sums, grad_in = lax.optimization_barrier((rounded(sums), grad_in))
    summed = rounded(row_sums(sums))
    summed, mixed_out = lax.optimization_barrier((summed, mixed_out))
    summed = lax.all_gather(summed, "dp", axis=0, tiled=True).astype(f32)
    out_sum = summed[:, :query_cols]
    qkv_sum = summed[:, main:]
    weights = jnp.concatenate([query_weight, key_weight, value_weight], 1).astype(f32)
    small_gain = jnp.sum(weights * qkv_sum, 1) / norm1_gain
    also = jnp.concatenate([of_two(summed[:, query_cols:main]), small_gain[:, None]], 1)
    also = also + lax.ppermute(also, "col", mirror)
    return (
        mixed_out,
        grad_in,
        also[:, experts + 1],
        qkv_sum[:, :query_cols],
        qkv_sum[:, query_cols : query_cols + key_cols],
        qkv_sum[:, query_cols + key_cols :],
        out_sum.T,
        also[:, experts],
        also[:, :experts],
        grad_gate,
        grad_up,
        grad_down,
    )


def solution(mesh):
    return jax.shard_map(
        per_device,
        mesh=mesh,
        in_specs=(
            P(("dp", "col"), "row"),
            P("row"),
            P("row", "col"),
            P("row", "col"),
            P("row", "col"),
            P("col", "row"),
            P("row"),
            P("row", None),
            P(None, "row", "col"),
            P(None, "row", "col"),
            P(None, "col", "row"),
            P("dp", None),
            P("dp", None),
            P(("dp", "col"), "row"),
        ),
        out_specs=(
            P(("dp", "col"), "row"),
            P(("dp", "col"), "row"),
            P("row"),
            P("row", "col"),
            P("row", "col"),
            P("row", "col"),
            P("col", "row"),
            P("row"),
            P("row", None),
            P("dp", "row", "col"),
            P("dp", "row", "col"),
            P("dp", "col", "row"),
        ),
        check_vma=False,
    )
```

```python
import functools

import jax
import jax.numpy as jnp
from jax import lax
from jax.experimental import pallas as pl
from jax.experimental.pallas import tpu as pltpu
from jax.sharding import PartitionSpec as P

HEAD_DIM = 64
LANES = 128

epsilon = 1e-06
rope_base = 10000.0
masked_score = -1e30

f32 = jnp.float32
bf16 = jnp.bfloat16

BIG = pltpu.CompilerParams(vmem_limit_bytes=56 * 1024 * 1024)


def dot(left, right):
    return lax.dot_general(left, right, (((1,), (0,)), ((), ())), preferred_element_type=f32)


def dot_nt(left, right):
    return lax.dot_general(left, right, (((1,), (1,)), ((), ())), preferred_element_type=f32)


def dot_tn(left, right):
    return lax.dot_general(left, right, (((0,), (0,)), ((), ())), preferred_element_type=f32)


def rope_tables(seq_len):
    midpoint = HEAD_DIM // 2
    frequency = rope_base ** (-2.0 * jnp.arange(midpoint, dtype=f32) / HEAD_DIM)
    angles = jnp.arange(seq_len, dtype=f32)[:, None] * frequency[None, :]
    cosines, sines = jnp.cos(angles), jnp.sin(angles)
    return (
        jnp.tile(cosines, (1, LANES // midpoint)),
        jnp.tile(jnp.concatenate([-sines, sines], 1), (1, LANES // HEAD_DIM)),
    )


def partner(tile):
    lane = lax.broadcasted_iota(jnp.int32, tile.shape, 1)
    half = HEAD_DIM // 2
    return jnp.where(
        (lane % HEAD_DIM) < half,
        pltpu.roll(tile, LANES - half, 1),
        pltpu.roll(tile, half, 1),
    )


def spread_pair(tile):
    tile = tile.astype(f32)
    lane = lax.broadcasted_iota(jnp.int32, tile.shape, 1)
    swapped = pltpu.roll(tile, HEAD_DIM, 1)
    low = lane < HEAD_DIM
    return (
        jnp.where(low, tile, swapped).astype(bf16),
        jnp.where(low, swapped, tile).astype(bf16),
    )


def split_heads(tile):
    lane = lax.broadcasted_iota(jnp.int32, tile.shape, 1)
    low = lane < HEAD_DIM
    zero = jnp.zeros_like(tile)
    return jnp.where(low, tile, zero), jnp.where(low, zero, tile)


def block_mask(seg_col, seg_row, start, rows, keys):
    row = lax.broadcasted_iota(jnp.int32, (rows, keys), 0) + start
    key = lax.broadcasted_iota(jnp.int32, (rows, keys), 1)
    return (key <= row) & (seg_col[start : start + rows, :] == seg_row[:, :keys])


def attend_kernel(
    query_in, key_in, value_in, cos_ref, sin_ref, col_ref, row_ref,
    query_out, key_out, value_out, heads_out, sums_out, *, block
):
    seq_len = query_in.shape[0]
    cosines, sines = cos_ref[...], sin_ref[...]
    key = key_in[...]
    key_low = (key * cosines + partner(key) * sines).astype(bf16)
    key_out[...] = key_low
    value_low = value_in[...].astype(bf16)
    value_out[...] = value_low
    keys, values = spread_pair(key_low), spread_pair(value_low)
    lane = lax.broadcasted_iota(jnp.int32, (block, LANES), 1)
    scale = 1.0 / HEAD_DIM
    for group in range(2):
        cols = slice(group * LANES, (group + 1) * LANES)
        query = query_in[:, cols]
        query_low = (query * cosines + partner(query) * sines).astype(bf16)
        query_out[:, cols] = query_low
        parts = split_heads(query_low)
        value_parts = split_heads(values[group])
        for start in range(0, seq_len, block):
            reach = start + block
            mask = block_mask(col_ref[...], row_ref[...], start, block, reach)
            total = jnp.zeros((block, LANES), f32)
            for head in range(2):
                scores = dot_nt(parts[head][start:reach], keys[group][:reach]) * scale
                scores = jnp.where(mask, scores, masked_score)
                top = jnp.max(scores, -1, keepdims=True)
                powers = jnp.exp(scores - top)
                mass = jnp.sum(powers, -1, keepdims=True)
                attention = (powers / mass).astype(bf16)
                total += dot(attention, value_parts[head][:reach])
                place = group * 2 + head
                sums = jnp.broadcast_to(top + jnp.log(mass), (block, LANES))
                if place == 0:
                    sums_out[start:reach, :] = sums
                else:
                    sums_out[start:reach, :] = jnp.where(
                        lane == place, sums, sums_out[start:reach, :]
                    )
            heads_out[start:reach, cols] = total.astype(bf16)


def attend_forward(raw, tables, seg_col, seg_row, kv_heads, block):
    seq_len = raw.shape[0]
    pairs = kv_heads // 2
    width = pairs * LANES
    spec = lambda cols, at: pl.BlockSpec((seq_len, cols), at)
    return pl.pallas_call(
        functools.partial(attend_kernel, block=block),
        grid=(pairs,),
        in_specs=[
            spec(2 * LANES, lambda i: (0, i)),
            spec(LANES, lambda i: (0, 2 * pairs + i)),
            spec(LANES, lambda i: (0, 3 * pairs + i)),
            spec(LANES, lambda i: (0, 0)),
            spec(LANES, lambda i: (0, 0)),
            pl.BlockSpec((seq_len, 1), lambda i: (0, 0)),
            pl.BlockSpec((1, seq_len), lambda i: (0, 0)),
        ],
        out_specs=[
            spec(2 * LANES, lambda i: (0, i)),
            spec(LANES, lambda i: (0, i)),
            spec(LANES, lambda i: (0, i)),
            spec(2 * LANES, lambda i: (0, i)),
            spec(LANES, lambda i: (0, i)),
        ],
        out_shape=[
            jax.ShapeDtypeStruct((seq_len, 2 * width), bf16),
            jax.ShapeDtypeStruct((seq_len, width), bf16),
            jax.ShapeDtypeStruct((seq_len, width), bf16),
            jax.ShapeDtypeStruct((seq_len, 2 * width), bf16),
            jax.ShapeDtypeStruct((seq_len, width), f32),
        ],
        compiler_params=BIG,
        name="attend_forward",
    )(raw, raw, raw, *tables, seg_col, seg_row)


def attend_back_kernel(
    query_in, key_in, value_in, sums_in, grad_in, cos_ref, sin_ref, col_ref, row_ref,
    query_out, key_out, value_out, key_sum, value_sum, *, block
):
    seq_len = query_in.shape[0]
    keys, values = spread_pair(key_in[...]), spread_pair(value_in[...])
    lane = lax.broadcasted_iota(jnp.int32, (seq_len, LANES), 1)
    low = lane < HEAD_DIM
    scale = 1.0 / HEAD_DIM
    folded = []
    for group in range(2):
        cols = slice(group * LANES, (group + 1) * LANES)
        query_parts = split_heads(query_in[:, cols])
        grad_parts = split_heads(grad_in[:, cols])
        key_parts = split_heads(keys[group])
        key_sum[...] = jnp.zeros_like(key_sum)
        value_sum[...] = jnp.zeros_like(value_sum)
        for start in range(0, seq_len, block):
            reach = start + block
            rows = slice(start, reach)
            mask = block_mask(col_ref[...], row_ref[...], start, block, reach)
            total = jnp.zeros((block, LANES), f32)
            for head in range(2):
                place = group * 2 + head
                query, grad = query_parts[head][rows], grad_parts[head][rows]
                scores = dot_nt(query, keys[group][:reach]) * scale
                powers = jnp.exp(scores - sums_in[rows, place : place + 1])
                attention = jnp.where(mask, powers, 0.0)
                value_sum[:reach, :] += dot_tn(attention.astype(bf16), grad)
                grad_probs = dot_nt(grad, values[group][:reach])
                inner = jnp.sum(grad_probs * attention, -1, keepdims=True)
                grad_scores = (attention * (grad_probs - inner) * scale).astype(bf16)
                key_sum[:reach, :] += dot_tn(grad_scores, query)
                total += dot(grad_scores, key_parts[head][:reach])
            cosines, sines = cos_ref[rows, :], sin_ref[rows, :]
            query_out[rows, cols] = (total * cosines - partner(total) * sines).astype(bf16)
        grad_key, grad_value = key_sum[...], value_sum[...]
        folded.append(
            (
                grad_key + pltpu.roll(grad_key, HEAD_DIM, 1),
                grad_value + pltpu.roll(grad_value, HEAD_DIM, 1),
            )
        )
    grad_key = jnp.where(low, folded[0][0], folded[1][0])
    grad_value = jnp.where(low, folded[0][1], folded[1][1])
    key_out[...] = (grad_key * cos_ref[...] - partner(grad_key) * sin_ref[...]).astype(bf16)
    value_out[...] = grad_value.astype(bf16)


def in_vmem(count):
    return [pl.BlockSpec(memory_space=pltpu.VMEM) for _ in range(count)]


def weight_products_kernel(mid_ref, heads_ref, small_ref, left_ref, *refs):
    *right_refs, out_ref = refs
    start = heads_ref.shape[1]
    out_ref[:, :start] = dot_tn(mid_ref[...], heads_ref[...]).astype(bf16)
    out_ref[:, start : start + LANES] = small_ref[...]
    start += LANES
    for right in right_refs:
        stop = start + right.shape[1]
        out_ref[:, start:stop] = dot_tn(left_ref[...], right[...]).astype(bf16)
        start = stop


def weight_products(mid, heads, small, left, rights):
    cols = heads.shape[1] + LANES + sum(right.shape[1] for right in rights)
    return pl.pallas_call(
        weight_products_kernel,
        in_specs=in_vmem(4 + len(rights)),
        out_specs=in_vmem(1)[0],
        out_shape=jax.ShapeDtypeStruct((left.shape[1], cols), bf16),
        compiler_params=BIG,
        name="weight_products",
    )(mid, heads, small, left, *rights)


def attend_backward(query, key, value, sums, grad, tables, seg_col, seg_row, block):
    seq_len = query.shape[0]
    width = key.shape[1]
    pairs = width // LANES
    spec = lambda cols, at: pl.BlockSpec((seq_len, cols), at)
    here = lambda i: (0, i)
    first = lambda i: (0, 0)
    return pl.pallas_call(
        functools.partial(attend_back_kernel, block=block),
        grid=(pairs,),
        in_specs=[
            spec(2 * LANES, here),
            spec(LANES, here),
            spec(LANES, here),
            spec(LANES, here),
            spec(2 * LANES, here),
            spec(LANES, first),
            spec(LANES, first),
            pl.BlockSpec((seq_len, 1), first),
            pl.BlockSpec((1, seq_len), first),
        ],
        out_specs=[spec(2 * LANES, here), spec(LANES, here), spec(LANES, here)],
        out_shape=[
            jax.ShapeDtypeStruct((seq_len, 2 * width), bf16),
            jax.ShapeDtypeStruct((seq_len, width), bf16),
            jax.ShapeDtypeStruct((seq_len, width), bf16),
        ],
        scratch_shapes=[pltpu.VMEM((seq_len, LANES), f32), pltpu.VMEM((seq_len, LANES), f32)],
        compiler_params=BIG,
        name="attend_backward",
    )(query, key, value, sums, grad, *tables, seg_col, seg_row)


def place_rows_of(place_ref, starts_ref, which, tokens, window, capacity):
    start = starts_ref[which]
    start = pl.multiple_of(jnp.minimum(start - start % 16, capacity - window), 16)
    slots = lax.broadcasted_iota(jnp.int32, (window, tokens), 0) + start
    return start, jnp.where(slots == place_ref, 1.0, 0.0).astype(bf16)


def store_at(step, refs, value):
    for index, ref in enumerate(refs):

        @pl.when(step == index)
        def _():
            ref[...] = value


def dispatch_two_kernel(starts_ref, place_ref, *refs, count):
    blocks, out_refs, total = refs[: -1 - count], refs[-1 - count : -1], refs[-1]
    tokens = blocks[0].shape[0]
    capacity = total.shape[0]
    window = tokens + 16
    expert = pl.program_id(0)
    total[...] = jnp.zeros_like(total)
    for index, block in enumerate(blocks):
        start, chosen = place_rows_of(
            place_ref[0, :, index * tokens : (index + 1) * tokens],
            starts_ref,
            expert * len(blocks) + index,
            tokens,
            window,
            capacity,
        )
        total[pl.ds(start, window), :] += dot(chosen, block[...])
    store_at(expert, out_refs, total[...].astype(bf16))


def dispatch_grads_kernel(starts_ref, place_ref, stack_ref, member_ref, *refs, block):
    *out_refs, total = refs
    parts, tokens, width = stack_ref.shape
    capacity = total.shape[0]
    window = block + 16
    expert = pl.program_id(0)
    total[...] = jnp.zeros_like(total)
    steps = tokens // block
    for step in range(steps):
        rows = slice(step * block, (step + 1) * block)
        start, chosen = place_rows_of(
            place_ref[0, :, rows], starts_ref, expert * steps + step, block, window, capacity
        )
        values = jnp.concatenate(
            [stack_ref[part, rows, :] for part in range(parts)] + [member_ref[rows, :]], 1
        )
        total[pl.ds(start, window), :] += dot(chosen, values)
    store_at(expert, out_refs, total[...].astype(bf16))


def dispatch(kernel, name, starts, places, arrays, capacity, width):
    count, _, tokens = places.shape
    whole = lambda array: pl.BlockSpec(array.shape, lambda i: (0,) * array.ndim)
    return pl.pallas_call(
        kernel,
        grid=(count,),
        in_specs=[
            pl.BlockSpec(memory_space=pltpu.SMEM),
            pl.BlockSpec((1, 1, tokens), lambda i: (i, 0, 0)),
        ]
        + [whole(array) for array in arrays],
        out_specs=[pl.BlockSpec((capacity, width), lambda i: (0, 0))] * count,
        out_shape=[jax.ShapeDtypeStruct((capacity, width), bf16)] * count,
        scratch_shapes=[pltpu.VMEM((capacity, width), f32)],
        compiler_params=BIG,
        name=name,
    )(starts, places, *arrays)


def dispatch_two(starts, places, blocks, capacity):
    count = places.shape[0]
    kernel = functools.partial(dispatch_two_kernel, count=count)
    width = blocks[0].shape[1]
    return dispatch(kernel, "dispatch_tokens", starts, places, blocks, capacity, width)


def dispatch_grads(starts, places, stack, members, capacity, block):
    kernel = functools.partial(dispatch_grads_kernel, block=block)
    width = stack.shape[0] * stack.shape[2] + LANES
    return dispatch(
        kernel, "dispatch_grads", starts, places, [stack, members], capacity, width
    )


def gather_back(starts_ref, place_ref, value_refs, which, capacity):
    tokens = place_ref.shape[0]
    window = 2 * tokens
    count = len(value_refs)
    total = None
    for expert, values_ref in enumerate(value_refs):
        start = starts_ref[which * count + expert]
        start = pl.multiple_of(jnp.minimum(start - start % 16, capacity - window), 16)
        slots = lax.broadcasted_iota(jnp.int32, (tokens, window), 1) + start
        chosen = jnp.where(slots == place_ref[:, expert : expert + 1], 1.0, 0.0).astype(bf16)
        term = dot(chosen, values_ref[pl.ds(start, window), :])
        total = term if total is None else total + term
    return total


def combine_kernel(starts_ref, place_ref, *refs, capacity, count):
    value_refs = refs[:count]
    own_ref, away_ref = refs[-2:]
    step = pl.program_id(0)
    half = pl.num_programs(0) // 2
    pieces = place_ref.shape[0] // LANES
    for piece in range(pieces):
        rows = slice(piece * LANES, (piece + 1) * LANES)
        total = gather_back(
            starts_ref, place_ref[rows, :], value_refs, step * pieces + piece, capacity
        ).astype(bf16)

        @pl.when(step < half)
        def _():
            away_ref[0, rows, :] = total

        @pl.when(step >= half)
        def _():
            own_ref[0, rows, :] = total


def combine(starts, places, values, block, after):
    tokens = places.shape[0]
    capacity, width = values[0].shape
    half = tokens // block // 2
    out = jax.ShapeDtypeStruct((half, block, width), bf16)
    return pl.pallas_call(
        functools.partial(combine_kernel, capacity=capacity, count=len(values)),
        grid=(2 * half,),
        in_specs=[
            pl.BlockSpec(memory_space=pltpu.SMEM),
            pl.BlockSpec((block, LANES), lambda i: (i, 0)),
        ]
        + [pl.BlockSpec((capacity, width), lambda i: (0, 0)) for _ in values]
        + [pl.BlockSpec(memory_space=pl.ANY) for _ in after],
        out_specs=[
            pl.BlockSpec((1, block, width), lambda i: (jnp.maximum(i - half, 0), 0, 0)),
            pl.BlockSpec((1, block, width), lambda i: (jnp.minimum(i, half - 1), 0, 0)),
        ],
        out_shape=[out, out],
        compiler_params=BIG,
        name="combine_rows",
    )(starts, places, *values, *after)


def combine_add_kernel(own_ref, starts_ref, place_ref, add_ref, *refs, capacity):
    *value_refs, out_ref = refs
    step = pl.program_id(0)
    factor = jnp.where(step == own_ref[0], 1.0, 0.0)
    parts, block, width = out_ref.shape
    pieces = block // LANES
    for piece in range(pieces):
        rows = slice(piece * LANES, (piece + 1) * LANES)
        total = gather_back(
            starts_ref, place_ref[rows, :], value_refs, step * pieces + piece, capacity
        )
        total += add_ref[rows, :] * factor
        for part in range(parts):
            out_ref[part, rows, :] = total[:, part * width : (part + 1) * width].astype(bf16)


def combine_add(own, starts, places, values, addition, parts):
    tokens = places.shape[0]
    capacity, width = values[0].shape
    block = addition.shape[0]
    return pl.pallas_call(
        functools.partial(combine_add_kernel, capacity=capacity),
        grid=(tokens // block,),
        in_specs=[
            pl.BlockSpec(memory_space=pltpu.SMEM),
            pl.BlockSpec(memory_space=pltpu.SMEM),
            pl.BlockSpec((block, LANES), lambda i: (i, 0)),
            pl.BlockSpec((block, width), lambda i: (0, 0)),
        ]
        + [pl.BlockSpec((capacity, width), lambda i: (0, 0)) for _ in values],
        out_specs=pl.BlockSpec((parts, block, width // parts), lambda i: (0, i, 0)),
        out_shape=jax.ShapeDtypeStruct((parts, tokens, width // parts), bf16),
        compiler_params=BIG,
        name="combine_rows_add",
    )(own, starts, places, addition, *values)


def weight_blocks(row_count, col_count, part, hidden_cols):
    for row in range(row_count):
        for col in range(col_count):
            rows = slice(row * part, (row + 1) * part)
            cols = slice(col * part, (col + 1) * part)
            above = slice(hidden_cols + col * part, hidden_cols + (col + 1) * part)
            yield row * col_count + col, rows, cols, above


def expert_kernel(
    weight_ref, router_ref, pick_ref, *refs, groups, row_count, col_count
):
    slot_refs, grad_refs = refs[:groups], refs[groups : 2 * groups]
    out_refs, back_a_refs, back_b_refs = (
        refs[at * groups : (at + 1) * groups] for at in (2, 3, 4)
    )
    save_refs = refs[5 * groups : 6 * groups]
    up_ref, down_ref, slot_ref, grad_ref = refs[6 * groups :]
    step = pl.program_id(0) * pl.num_programs(1) + pl.program_id(1)
    width = slot_ref.shape[1]
    split = back_b_refs[0].shape[1]
    for group in range(groups):

        @pl.when(pl.program_id(0) == group)
        def _():
            slot_ref[...] = slot_refs[group][...]
            grad_ref[...] = grad_refs[group][...]

    hidden_cols = down_ref.shape[0]
    part = weight_ref.shape[2]

    @pl.when(step == 0)
    def _():
        for cell, rows, cols, above in weight_blocks(row_count, col_count, part, hidden_cols):
            up_ref[rows, cols] = weight_ref[cell, :part, :]
            up_ref[rows, above] = weight_ref[cell, part : 2 * part, :]
            down_ref[cols, rows] = weight_ref[cell, 2 * part :, :]

    slots = slot_ref[...]
    grads = grad_ref[:, :width].astype(f32)
    member = grad_ref[:, width:].astype(f32) > 0.5
    logits = jnp.where(member, dot(slots, router_ref[...]), masked_score)
    top = jnp.max(logits, -1, keepdims=True)
    powers = jnp.where(member, jnp.exp(logits - top), 0.0)
    mass = jnp.sum(powers, -1, keepdims=True)
    pick = pick_ref[...]
    gate = jnp.sum(powers * pick[0:1, :], -1, keepdims=True) / jnp.maximum(mass, 1e-30)
    both = dot(slots, up_ref[...])
    gate_part, up_part = both[:, :hidden_cols], both[:, hidden_cols:]
    sigmoid = 1.0 / (1.0 + jnp.exp(-gate_part))
    silu = gate_part * sigmoid
    hidden = (silu * up_part).astype(bf16)
    result = dot(hidden, down_ref[...])
    scaled = (result * gate).astype(bf16)
    dots = jnp.sum(result * grads, -1, keepdims=True)
    dots_high = dots.astype(bf16).astype(f32)
    dots_low = dots - dots_high
    split_dots = (dots_high * pick[0:1, :] + dots_low * pick[1:2, :]).astype(bf16)
    grad_expert = (grads * gate).astype(bf16)
    grad_hidden = dot_nt(grad_expert, down_ref[...])
    grad_pair = jnp.concatenate(
        [
            grad_hidden * up_part * sigmoid * (1.0 + gate_part * (1.0 - sigmoid)),
            grad_hidden * silu,
        ],
        1,
    ).astype(bf16)
    back = dot_nt(grad_pair, up_ref[...]).astype(bf16)
    for group in range(groups):

        @pl.when(pl.program_id(0) == group)
        def _():
            out_refs[group][...] = scaled
            back_a_refs[group][:, :LANES] = split_dots
            back_a_refs[group][:, LANES:] = back[:, : width - split]
            back_b_refs[group][...] = back[:, width - split :]
            save_refs[group][:, :hidden_cols] = hidden
            save_refs[group][:, hidden_cols : hidden_cols + width] = grad_expert
            save_refs[group][:, hidden_cols + width :] = grad_pair


def expert_grads_kernel(*refs, groups, row_count, col_count):
    slot_refs, save_refs, out_ref = refs[:groups], refs[groups : 2 * groups], refs[2 * groups]
    part = out_ref.shape[2]
    width = slot_refs[0].shape[1]
    hidden_cols = col_count * part
    first_pair = hidden_cols + width

    def product(lefts, left_cols, rights, right_cols):
        terms = [
            dot_tn(left[:, left_cols], right[:, right_cols]) for left, right in zip(lefts, rights)
        ]
        return sum(terms).astype(bf16)

    for cell, rows, cols, above in weight_blocks(row_count, col_count, part, hidden_cols):
        for place, pair in enumerate((cols, above)):
            pair = slice(first_pair + pair.start, first_pair + pair.stop)
            out_ref[cell, place * part : (place + 1) * part, :] = product(
                slot_refs, rows, save_refs, pair
            )
        out = slice(hidden_cols + rows.start, hidden_cols + rows.stop)
        out_ref[cell, 2 * part :, :] = product(save_refs, cols, save_refs, out)


def expert_grads(slots, saved, shape, row_count, col_count):
    groups = len(slots)
    return pl.pallas_call(
        functools.partial(
            expert_grads_kernel, groups=groups, row_count=row_count, col_count=col_count
        ),
        in_specs=in_vmem(2 * groups),
        out_specs=in_vmem(1)[0],
        out_shape=jax.ShapeDtypeStruct(shape, bf16),
        compiler_params=BIG,
        name="expert_grads",
    )(*slots, *saved)


def run_expert(slots, grads, weights, router, pick, steps, row_count, col_count):
    groups = len(slots)
    capacity, width = slots[0].shape
    rest = grads[0].shape[1]
    half = width // 2
    block = capacity // steps
    hidden_cols = weights.shape[2] * col_count
    kept = 3 * hidden_cols + width
    whole = lambda shape: pl.BlockSpec(shape, lambda i, j: (0,) * len(shape))

    def some(cols):
        def spec(group):
            return pl.BlockSpec(
                (block, cols),
                lambda i, j: (
                    jnp.where(i < group, 0, jnp.where(i > group, steps - 1, j)),
                    0,
                ),
            )

        return [spec(group) for group in range(groups)]

    shapes = lambda cols: [jax.ShapeDtypeStruct((capacity, cols), bf16)] * groups
    outs = pl.pallas_call(
        functools.partial(
            expert_kernel, groups=groups, row_count=row_count, col_count=col_count
        ),
        grid=(groups, steps),
        in_specs=[whole(weights.shape), whole(router.shape), whole(pick.shape)]
        + some(width)
        + some(rest),
        out_specs=some(width) + some(half + LANES) + some(half) + some(kept),
        out_shape=shapes(width)
        + shapes(half + LANES)
        + shapes(half)
        + shapes(kept),
        scratch_shapes=[
            pltpu.VMEM((width, 2 * hidden_cols), bf16),
            pltpu.VMEM((hidden_cols, width), bf16),
            pltpu.VMEM((block, width), bf16),
            pltpu.VMEM((block, rest), bf16),
        ],
        compiler_params=BIG,
        name="expert_pass",
    )(weights, router, pick, *slots, *grads)
    return (
        outs[:groups],
        outs[groups : 2 * groups],
        outs[2 * groups : 3 * groups],
        outs[3 * groups :],
    )


def spread_kernel(block_ref, *out_refs):
    part = out_refs[0].shape[1]
    for index, out_ref in enumerate(out_refs):
        out_ref[0] = block_ref[0, index * part : (index + 1) * part, :].astype(f32)


def spread_blocks(blocks, count):
    cells, rows, cols = blocks.shape
    part = rows // count
    return pl.pallas_call(
        spread_kernel,
        grid=(cells,),
        in_specs=[pl.BlockSpec((1, rows, cols), lambda i: (i, 0, 0))],
        out_specs=[pl.BlockSpec((1, part, cols), lambda i: (i, 0, 0))] * count,
        out_shape=[jax.ShapeDtypeStruct((cells, part, cols), f32)] * count,
        compiler_params=BIG,
        name="spread_blocks",
    )(blocks)


def norm_back(grad, values, inv_rms, gain):
    scaled = grad * gain
    inner = jnp.mean(scaled * values, -1, keepdims=True)
    grad_gain = jnp.sum(grad * values * inv_rms, 0)
    return (inv_rms * scaled - values * inv_rms * inv_rms * inv_rms * inner, grad_gain)


def inverse_rms(values):
    return lax.rsqrt(jnp.mean(values * values, -1, keepdims=True) + epsilon)


def running_count(member):
    tokens, cols = member.shape
    chunk = LANES
    parts = member.reshape(tokens // chunk, chunk, cols)
    lower = jnp.tril(jnp.ones((chunk, chunk), f32))
    inside = jnp.einsum("ij,bjc->bic", lower, parts, preferred_element_type=f32)
    sums = jnp.sum(parts, 1)
    blocks = tokens // chunk
    before = jnp.sum(
        jnp.where(
            jnp.arange(blocks)[:, None, None] > jnp.arange(blocks)[None, :, None],
            sums[None, :, :],
            0.0,
        ),
        1,
    )
    return (inside + before[:, None, :]).reshape(tokens, cols).astype(jnp.int32)


def per_device(
    hidden_in,
    norm1_gain,
    query_weight,
    key_weight,
    value_weight,
    output_weight,
    norm2_gain,
    router_weight,
    gate_weight,
    up_weight,
    down_weight,
    segment_ids,
    expert_ids,
    grad_out,
):
    dp_count = lax.axis_size("dp")
    row_count = lax.axis_size("row")
    col_count = lax.axis_size("col")
    dp_at, row_at, col_at = (lax.axis_index(name) for name in ("dp", "row", "col"))
    cell = row_at * col_count + col_at
    cells = row_count * col_count
    local_rows, local_width = hidden_in.shape
    group, chosen = expert_ids.shape
    width = local_width * row_count
    experts = gate_weight.shape[0]
    hidden_part = gate_weight.shape[2]
    hidden_cols = hidden_part * col_count
    capacity = group * chosen * 5 // (4 * experts)
    sequences, seq_len = segment_ids.shape
    own_rows = seq_len // col_count
    query_cols, key_cols = query_weight.shape[1], key_weight.shape[1]
    kv_heads = key_cols // HEAD_DIM
    block = seq_len // 2
    spread = experts // cells
    copies = dp_count // spread
    per_dp = experts // dp_count
    assert sequences == row_count and spread * cells == experts and copies * spread == dp_count
    spread_at = dp_at % spread
    if copies == 1:
        far = None
    else:
        far = [[i * spread + j for i in range(copies)] for j in range(spread)]

    def exchange(arrays):
        return [over_dp(array, turn) for turn, array in enumerate(arrays)]

    def by_cell(array):
        lead = array.shape[:-1]
        split = array.reshape(lead + (copies, spread, per_dp))
        return jnp.swapaxes(split, -3, -2).reshape(lead + (spread, cells))

    per_col = sequences // col_count
    part_at = (row_at // col_count) * col_count + col_at
    sequence_of = lambda row: (row % col_count) * per_col + row // col_count
    block_of = lambda row, col: sequence_of(row) * col_count + col
    own_block = block_of(row_at, col_at)

    def rounds():
        for turn in range(row_count):
            there, back = [], []
            for row in range(row_count):
                for col in range(col_count):
                    part = (row - turn) % row_count
                    other = ((part // col_count) * col_count + col) * col_count + part % col_count
                    there.append((row * col_count + col, other))
                    back.append((other, row * col_count + col))
            yield turn, there, back

    def to_sequences(array):
        parts = array.reshape(per_col, seq_len, local_width)
        got = []
        for turn, there, _ in rounds():
            part = (row_at - turn) % row_count
            own = lax.dynamic_index_in_dim(parts, part // col_count, 0, keepdims=False)
            got.append(lax.ppermute(own, ("row", "col"), there))
        got = jnp.stack(got)
        return jnp.concatenate(
            [
                lax.dynamic_index_in_dim(got, (row - part_at) % row_count, 0, keepdims=False)
                for row in range(row_count)
            ],
            1,
        )

    def from_sequences(array):
        parts = array.reshape(seq_len, row_count, local_width).transpose(1, 0, 2)
        got = []
        for turn, _, back in rounds():
            own = lax.dynamic_index_in_dim(
                parts, (turn + part_at) % row_count, 0, keepdims=False
            )
            got.append(lax.ppermute(own, ("row", "col"), back).astype(f32))
        total = []
        for index in range(per_col):
            total.append(
                sum(
                    jnp.where(((row_at - turn) % row_count) // col_count == index, got[turn], 0.0)
                    for turn in range(row_count)
                )
            )
        return jnp.concatenate(total, 0)

    own_start = col_at * own_rows
    mirror = [(col, col_count - 1 - col) for col in range(col_count)]

    def sum_halves(array):
        parts = array.reshape(col_count, own_rows, array.shape[1])
        away = lax.dynamic_index_in_dim(parts, 1 - col_at, 0, keepdims=False).astype(bf16)
        own = lax.dynamic_index_in_dim(parts, col_at, 0, keepdims=False)
        return own + lax.ppermute(away, "col", mirror).astype(f32)

    def join_halves(array):
        other = lax.ppermute(array, "col", mirror)
        first = col_at == 0
        return jnp.concatenate(
            [jnp.where(first, array, other), jnp.where(first, other, array)], 0
        )

    def in_terms(array):
        terms = []
        for _ in range(3):
            terms.append(array.astype(bf16))
            array = array - terms[-1].astype(f32)
        return terms

    tokens_in = to_sequences(hidden_in)
    extras = jnp.concatenate(
        [router_weight, jnp.stack(in_terms(norm1_gain) + in_terms(norm2_gain), 1)], 1
    )
    def over_rows(array, turn):
        pairs = [(row, row ^ turn) for row in range(row_count)]
        return lax.ppermute(array, "row", pairs) if turn else array

    def over_dp(array, turn):
        pairs = [(at, at ^ turn) for at in range(dp_count)]
        return lax.ppermute(array, "dp", pairs) if turn else array

    def over_cells(array, turn):
        pairs = [(at, at ^ turn) for at in range(cells)]
        return lax.ppermute(array, ("row", "col"), pairs) if turn else array

    pick_from = lambda array, at: lax.dynamic_index_in_dim(array, at, 0, keepdims=False)

    def all_rows(array):
        share = local_width // spread
        own = lax.dynamic_slice_in_dim(array, spread_at * share, share, 0)
        rows = jnp.stack([over_rows(own, turn) for turn in range(row_count)])
        rows = jnp.stack([pick_from(rows, row_at ^ row) for row in range(row_count)])
        shares = jnp.stack([over_dp(rows, turn) for turn in range(spread)])
        ordered = jnp.stack([pick_from(shares, spread_at ^ at) for at in range(spread)], 1)
        return ordered.reshape(width, array.shape[1])

    qkv_cols = query_cols + 2 * key_cols
    first_weights = all_rows(
        jnp.concatenate(
            [
                query_weight,
                key_weight,
                value_weight,
                jnp.pad(extras, ((0, 0), (0, LANES - extras.shape[1]))),
            ],
            1,
        )
    )
    first_weights, out_late = lax.optimization_barrier((first_weights, output_weight))
    out_weight = all_rows(out_late.T)
    grad_stack = lax.all_gather(grad_out, ("row", "col"), axis=0, tiled=True).reshape(
        row_count, group, local_width
    )

    qkv_weight = first_weights[:, :qkv_cols]
    extras = first_weights[:, qkv_cols:]
    router_pad = jnp.where(jnp.arange(LANES)[None, :] < experts, extras, jnp.zeros((), bf16))
    router = extras[:, :experts]
    terms = extras[:, experts : experts + 6].astype(f32)
    gain_one = (terms[:, 0] + terms[:, 1] + terms[:, 2])[None, :]
    gain_two = (terms[:, 3] + terms[:, 4] + terms[:, 5])[None, :]
    def from_rows(array):
        return [over_rows(array, turn) for turn in range(row_count)]

    def from_columns(rows):
        return [block for row in rows for block in (row, lax.ppermute(row, "col", mirror))]

    member = jnp.any(
        expert_ids[:, :, None] == jnp.arange(experts, dtype=jnp.int32)[None, None, :], 1
    )
    mine = lax.dynamic_index_in_dim(
        by_cell(member.astype(f32)), cell, 2, keepdims=False
    )
    mine = jnp.concatenate(
        [lax.dynamic_slice_in_dim(mine, spread_at ^ turn, 1, 1) for turn in range(spread)], 1
    )
    places = jnp.where(mine > 0.5, running_count(mine) - 1, -1)
    first = running_count(mine) - mine.astype(jnp.int32)
    token_blocks = places.reshape(cells, own_rows, spread)
    first_blocks = first.reshape(cells, own_rows, spread)[:, ::LANES]
    pad_cols = lambda array: jnp.pad(
        array, ((0, 0), (0, LANES - spread)), constant_values=-1
    )
    arrival = [
        block_of(row_at ^ turn, col_at ^ side)
        for turn in range(row_count)
        for side in range(2)
    ]
    away_first = [arrival[1::2], arrival[0::2]]
    order = lambda array, cells_of: jnp.stack(
        [lax.dynamic_index_in_dim(array, at, 0, keepdims=False) for at in cells_of]
    )
    rows_of = lambda array: array.reshape(group, spread).T.reshape(spread, 1, group)
    places_two = rows_of(order(token_blocks, arrival))
    starts_two = order(first_blocks, arrival)[:, 0].T.reshape(-1)
    combined = away_first[0] + away_first[1]
    places_back = pad_cols(order(token_blocks, combined).reshape(group, spread))
    starts_back = order(first_blocks, combined).reshape(-1)
    places_all = pad_cols(places)
    starts_all = first_blocks.reshape(-1)
    places_grad = rows_of(places)
    starts_grad = first_blocks[:, 0].T.reshape(-1)
    member_pad = jnp.pad(member.astype(bf16), ((0, 0), (0, LANES - experts)))
    my_expert = ((cell // per_dp) * spread + spread_at) * per_dp + cell % per_dp
    lane = jnp.arange(LANES)[None, :]
    pick = jnp.concatenate(
        [
            (lane == my_expert).astype(f32),
            (lane == experts + my_expert).astype(f32),
            jnp.zeros((6, LANES), f32),
        ],
        0,
    )
    tables = rope_tables(seq_len)
    segments = lax.dynamic_index_in_dim(segment_ids, sequence_of(row_at), 0, keepdims=True)
    seg_col = segments.reshape(seq_len, 1)
    residual = tokens_in.astype(f32)
    inv_one = inverse_rms(residual)
    normed_one = (residual * inv_one * gain_one).astype(bf16)
    raw = dot(normed_one, qkv_weight)
    query_low, key_low, value_low, heads, log_sums = attend_forward(
        raw, tables, seg_col, segments, kv_heads, block
    )
    attended = dot_nt(heads, out_weight)
    middle = lax.dynamic_slice_in_dim(residual, own_start, own_rows, 0) + sum_halves(attended)
    inv_two = inverse_rms(middle)
    normed_two = (middle * inv_two * gain_two).astype(bf16)
    half = width // 2
    early = spread - 1
    grad_slots = exchange(
        dispatch_grads(starts_grad, places_grad, grad_stack, member_pad, capacity, own_rows)
    )
    normed_sent, *grad_slots[:2] = lax.optimization_barrier((normed_two, *grad_slots[:2]))
    blocks = from_columns(from_rows(normed_sent))
    blocks[0], *grad_slots = lax.optimization_barrier((blocks[0], *grad_slots))

    def own_share(weight):
        split = weight.reshape((copies, spread, per_dp) + weight.shape[1:])
        return lax.dynamic_index_in_dim(split, spread_at, 1, keepdims=False).reshape(
            (cells,) + weight.shape[1:]
        )

    shares = jnp.concatenate(
        [own_share(gate_weight), own_share(up_weight), own_share(down_weight)], 1
    )
    *blocks, shares = lax.optimization_barrier((*blocks, shares))
    expert_weights = lax.all_to_all(shares, ("row", "col"), 0, 0, tiled=True)

    slots = exchange(dispatch_two(starts_two, places_two, blocks, capacity))
    results, back_a, back_b, saved = run_expert(
        slots, grad_slots, expert_weights, router_pad, pick, 2, row_count, col_count
    )

    def to_cells(back, after):
        return combine(starts_back, places_back, back, own_rows, after)

    def half_sums(own, away):
        return [own[turn].astype(f32) + away[turn].astype(f32) for turn in range(row_count)]

    def row_parts(sums):
        return [over_rows(sums[turn].astype(bf16), turn) for turn in range(1, row_count)]

    back_a, saved = exchange(back_a), list(saved)
    back_b = exchange(back_b)
    *back_a[:2], saved[0] = lax.optimization_barrier((*back_a[:2], saved[0]))
    back_a[0], *back_b[:early] = lax.optimization_barrier((back_a[0], *back_b[:early]))
    grad_blocks = expert_grads(slots, saved, shares.shape, row_count, col_count)
    kept_a, away_a = to_cells(back_a, [grad_blocks])
    grad_got = lax.all_to_all(grad_blocks, ("row", "col"), 0, 0, tiled=True)
    away_a = lax.ppermute(away_a, "col", mirror)
    kept_b, away_b = to_cells(back_b, [])
    away_a, kept_b, away_b = lax.optimization_barrier((away_a, kept_b, away_b))
    away_b = lax.ppermute(away_b, "col", mirror)
    sums_a = half_sums(kept_a, away_a)
    parts_a = row_parts(sums_a)
    back_b[-1], *results = lax.optimization_barrier((back_b[-1], *results))
    results = exchange(results)
    away_b, parts_a = lax.optimization_barrier((away_b, parts_a))
    sums_b = half_sums(kept_b, away_b)
    parts_b = row_parts(sums_b)
    mixed_rows = combine_add(
        own_block.reshape(1), starts_all, places_all, results, middle, row_count
    )
    parts_b, mixed_rows = lax.optimization_barrier((parts_b, mixed_rows))
    own_a = sums_a[0] + sum(part.astype(f32) for part in parts_a)
    own_b = sums_b[0] + sum(part.astype(f32) for part in parts_b)

    if copies > 1:
        grad_got = lax.psum_scatter(
            grad_got, "dp", scatter_dimension=0, axis_index_groups=far, tiled=True
        )

    own_member = lax.dynamic_slice_in_dim(member, own_block * own_rows, own_rows, 0)
    logits = jnp.where(own_member, dot(normed_two, router), masked_score)
    powers = jnp.where(own_member, jnp.exp(logits - jnp.max(logits, -1, keepdims=True)), 0.0)
    gates = powers / jnp.sum(powers, -1, keepdims=True)
    extra = own_a[:, :LANES]
    grad_gates = extra[:, :experts] + extra[:, experts : 2 * experts]
    grad_logits = (
        gates * (grad_gates - jnp.sum(gates * grad_gates, -1, keepdims=True))
    ).astype(bf16)
    grad_router = dot_tn(normed_two, grad_logits)
    grad_two = jnp.concatenate([own_a[:, LANES:], own_b], 1) + dot_nt(grad_logits, router)
    grad_norm, grad_gain_two = norm_back(grad_two, middle, inv_two, gain_two)
    own_grad = (
        lax.dynamic_slice_in_dim(grad_stack, own_block * own_rows, own_rows, 1)
        .transpose(1, 0, 2)
        .reshape(own_rows, width)
    )
    grad_middle = own_grad.astype(f32) + grad_norm

    share_rows = local_width // dp_count
    by_share = lambda array: array.reshape(
        array.shape[0], row_count, dp_count, share_rows
    ).swapaxes(1, 2).reshape(array.shape)

    def dp_sums(stacked):
        parts = stacked.reshape(dp_count, row_count * share_rows, stacked.shape[1])
        parts = lax.all_to_all(parts, "dp", 0, 0, tiled=True)
        summed = jnp.sum(parts.astype(f32), 0)
        return summed.reshape(row_count, share_rows, stacked.shape[1])

    def row_sums(parts):
        parts = lax.all_to_all(parts, "row", 0, 0, tiled=True)
        return jnp.sum(parts.astype(f32), 0)

    def in_two(array):
        high = array.astype(bf16)
        low = (array - high.astype(f32)).astype(bf16)
        pad = ((0, 0),) * (array.ndim - 1) + ((0, LANES - 2 * array.shape[-1]),)
        return jnp.pad(jnp.concatenate([high, low], -1), pad)

    smalls = experts + 1
    of_two = lambda array: array[..., :smalls] + array[..., smalls : 2 * smalls]

    grad_mid = join_halves(grad_middle.astype(bf16))
    grad_mid, grad_got = lax.optimization_barrier((grad_mid, grad_got))
    grad_gate, grad_up, grad_down = spread_blocks(grad_got, 3)
    small = jnp.concatenate([grad_router, grad_gain_two[:, None]], 1)
    grad_heads = dot(grad_mid, out_weight).astype(bf16)
    grad_heads, mixed_rows = lax.optimization_barrier((grad_heads, mixed_rows))
    mixed_out = lax.psum_scatter(
        mixed_rows.reshape(cells * local_rows, local_width),
        ("row", "col"),
        scatter_dimension=0,
        tiled=True,
    )
    grad_qkv = attend_backward(
        query_low, key_low, value_low, log_sums, grad_heads, tables, seg_col, segments, block
    )
    small = in_two(by_share(small.T).T)
    sums = dp_sums(
        weight_products(by_share(grad_mid), heads, small, by_share(normed_one), grad_qkv)
    )
    grad_qkv = jnp.concatenate(grad_qkv, 1)
    grad_one = dot_nt(grad_qkv, qkv_weight)
    grad_part, _ = norm_back(grad_one, residual, inv_one, gain_one)
    at_own = lax.dynamic_slice_in_dim(grad_part, own_start, own_rows, 0) + grad_middle
    grad_part = lax.dynamic_update_slice_in_dim(grad_part, at_own, own_start, 0)
    grad_in = from_sequences(grad_part.astype(bf16))
    main = query_cols + LANES

    def rounded(sums):
        return jnp.concatenate(
            [
                sums[..., :query_cols].astype(bf16),
                in_two(of_two(sums[..., query_cols:main])),
                sums[..., main:].astype(bf16),
            ],
            -1,
        )

    sums, grad_in = lax.optimization_barrier((rounded(sums), grad_in))
    summed = rounded(row_sums(sums))
    summed, mixed_out = lax.optimization_barrier((summed, mixed_out))
    summed = lax.all_gather(summed, "dp", axis=0, tiled=True).astype(f32)
    out_sum = summed[:, :query_cols]
    qkv_sum = summed[:, main:]
    weights = jnp.concatenate([query_weight, key_weight, value_weight], 1).astype(f32)
    small_gain = jnp.sum(weights * qkv_sum, 1) / norm1_gain
    also = jnp.concatenate([of_two(summed[:, query_cols:main]), small_gain[:, None]], 1)
    also = also + lax.ppermute(also, "col", mirror)
    return (
        mixed_out,
        grad_in,
        also[:, experts + 1],
        qkv_sum[:, :query_cols],
        qkv_sum[:, query_cols : query_cols + key_cols],
        qkv_sum[:, query_cols + key_cols :],
        out_sum.T,
        also[:, experts],
        also[:, :experts],
        grad_gate,
        grad_up,
        grad_down,
    )


def solution(mesh):
    return jax.shard_map(
        per_device,
        mesh=mesh,
        in_specs=(
            P(("dp", "col"), "row"),
            P("row"),
            P("row", "col"),
            P("row", "col"),
            P("row", "col"),
            P("col", "row"),
            P("row"),
            P("row", None),
            P(None, "row", "col"),
            P(None, "row", "col"),
            P(None, "col", "row"),
            P("dp", None),
            P("dp", None),
            P(("dp", "col"), "row"),
        ),
        out_specs=(
            P(("dp", "col"), "row"),
            P(("dp", "col"), "row"),
            P("row"),
            P("row", "col"),
            P("row", "col"),
            P("row", "col"),
            P("col", "row"),
            P("row"),
            P("row", None),
            P("dp", "row", "col"),
            P("dp", "row", "col"),
            P("dp", "col", "row"),
        ),
        check_vma=False,
    )
```
